256 devices in a mesh: dp: 16 (over y, x), feat: 16 (over z, core).
Axes of the slice: x: 4, y: 4, z: 8, core: 2. Of those that a mesh axis runs over, the one named last changes fastest.
Arguments:
- features: bfloat16 [262144, 768], P('dp', 'feat'), may hold values from -6 to 6
- target_ids: int32 [131072], P('dp'), may hold values from 0 to 16383
- tile_index: int32 [1024, 4], P('dp'), may hold values from 0 to 127
- tile_count: int32 [1024], P('dp'), may hold values from 1 to 4, as said below
- tile_values: bfloat16 [1024, 4, 128, 128], P('dp'), may hold values from 0 to 0.088378906
- w_neigh: bfloat16 [768, 1024], P('feat'), may hold values from -0.21875 to 0.21875
- w_self: bfloat16 [768, 1024], P('feat'), may hold values from -0.21875 to 0.21875
- bias: float32 [1024], replicated, may hold values from -3 to 3
- cotangent: bfloat16 [131072, 1024], P(('dp', 'feat')), may hold values from -0.125 to 0.125
Outputs:
- activation: bfloat16 [131072, 1024], P(('dp', 'feat'))
- grad_neigh: float32 [768, 1024], P('feat', 'dp')
- grad_self: float32 [768, 1024], P('feat', 'dp')
The draws below stay inside these ranges and needn't reach their ends.
Inputs may be any that keep to these rules, and one draw needn't show every extreme that they name: `tile_count`: in every replica some target block has all 4 slots live. `tile_index`: source blocks may repeat within a target block. `target_ids`: target rows may repeat.
All inputs are finite; a program needn't handle non-finite values.
Results may differ from the reference program's by a relative error of at most 0.0053.
Values may be sent and summed in bfloat16 or wider, within the bound.
No kernel may reach another device: no remote copies, remote signals or barrier semaphores. Data moves between devices by JAX's collectives and lax.ppermute only.
A program may use at most 128 MiB of HBM per device.

```python
import jax
import jax.numpy as jnp
from jax import lax

IN_WIDTH = 768
HID_WIDTH = 1024
TILE = 128
SLOTS = 4
TGT_BLK = 64
SRC_BLK = 128
TGT_REP = 8192
SRC_REP = 16384
TARGETS = 131072
SOURCES = 262144
BLOCKS = 1024
N_DP = 16


def draw_tile_count(key, part):
    key = jax.random.fold_in(key, 11)
    first, second = jax.random.split(key)
    counts = jax.random.randint(first, (BLOCKS,), 1, SLOTS + 1, dtype=jnp.int32)
    chosen = jax.random.randint(second, (BLOCKS // TGT_BLK,), 0, TGT_BLK, dtype=jnp.int32)
    rows_all = jnp.arange(BLOCKS, dtype=jnp.int32)
    replica_of = rows_all // TGT_BLK
    full_block = rows_all % TGT_BLK == chosen[replica_of]
    return jnp.where(full_block, jnp.int32(SLOTS), counts)


def touch_ends(drawn, own_key, least, largest):
    longest = drawn.shape.index(max(drawn.shape))
    spots = []
    for shift in (0, 1):
        where = [jax.random.randint(jax.random.fold_in(own_key, axis), (), 0, length) for axis, length in enumerate(drawn.shape)]
        where[longest] = (where[longest] + shift) % drawn.shape[longest]
        spots.append(tuple(where))
    return drawn.at[spots[0]].set(least).at[spots[1]].set(largest)


def strengthened(entries, rng, source, target, shards_of, factor):
    def block_of(axis_at):
        return (jnp.arange(entries.shape[axis_at]) // (entries.shape[axis_at] // shards_of)).reshape((-1,) + (1,) * (entries.ndim - 1 - axis_at))

    near = jax.random.permutation(rng, shards_of)[block_of(target)]
    far = (block_of(target) + shards_of // 2) % shards_of
    return jnp.where((block_of(source) == near) | (block_of(source) == far), factor * entries, entries)


def levels(own_key, extent, pieces, least, top_value):
    def one(axis_at, parts):
        draws = jax.random.uniform(jax.random.fold_in(jax.random.fold_in(own_key, 6), axis_at), (parts,), jnp.float32, least / len(pieces), top_value / len(pieces))
        return jnp.repeat(jnp.exp(draws), extent[axis_at] // parts).reshape((-1,) + (1,) * (len(extent) - axis_at - 1))

    loudness = one(*pieces[0])
    for cut in pieces[1:]:
        loudness = loudness * one(*cut)
    return loudness


def noise(key, dims, spread, bound, cuts=(), held_as=jnp.bfloat16):
    drawn = jax.random.normal(key, dims, jnp.float32) * spread
    if len(cuts) > 0:
        drawn = levels(key, dims, cuts, -0.22, 0.18) * drawn
    return jnp.clip(drawn, min=-bound, max=bound).astype(held_as)


def heavy_noise(stream_key, dims, deviation, limit, pieces, heavy, kind=jnp.bfloat16):
    array = deviation * jax.random.normal(stream_key, dims, jnp.float32)
    if pieces:
        array = array * levels(stream_key, dims, pieces, -0.22, 0.18)
    return jnp.clip(strengthened(array, jax.random.fold_in(stream_key, 3), *heavy), -limit, limit).astype(kind)


def setup_inputs(seed: int = 0) -> dict:
    keys = jax.random.split(jax.random.key(seed), 10)
    return {
        "features": noise(keys[0], (SOURCES, IN_WIDTH), 1.0, 6.0, ((0, 16), (1, 16))),
        "target_ids": touch_ends(jax.random.randint(keys[1], (TARGETS,), 0, SRC_REP), jax.random.fold_in(keys[1], 1), 0, SRC_REP - 1).astype(jnp.int32),
        "tile_index": touch_ends(jax.random.randint(keys[2], (BLOCKS, SLOTS), 0, SRC_BLK), jax.random.fold_in(keys[2], 1), 0, SRC_BLK - 1).astype(jnp.int32),
        "tile_count": draw_tile_count(jax.random.fold_in(keys[9], 71), 0),
        "tile_values": jnp.clip(0.088378906 * jax.random.uniform(keys[4], (BLOCKS, SLOTS, TILE, TILE), jnp.float32) ** levels(keys[4], (BLOCKS, SLOTS, TILE, TILE), ((0, 16),), -0.2, 0.2), 0.0, 0.088378906).astype(jnp.bfloat16),
        "w_neigh": noise(keys[5], (IN_WIDTH, HID_WIDTH), IN_WIDTH ** -0.5, 0.21875, ((0, 16),)),
        "w_self": noise(keys[6], (IN_WIDTH, HID_WIDTH), IN_WIDTH ** -0.5, 0.21875, ((0, 16),)),
        "bias": noise(keys[7], (HID_WIDTH,), 0.5, 3.0, (), jnp.float32),
        "cotangent": heavy_noise(keys[8], (TARGETS, HID_WIDTH), (2.0 / TARGETS ** 0.5), 0.125, ((0, 256),), (0, 1, 256, 6.0)),
    }


def smooth(value):
    return jax.nn.gelu(value, approximate=True)

def reference(features, target_ids, tile_index, tile_count, tile_values, w_neigh, w_self, bias, cotangent):
    feat_rep = features.reshape(N_DP, SRC_REP, IN_WIDTH)
    ids_rep = target_ids.reshape(N_DP, TGT_REP)
    index_rep = tile_index.reshape(N_DP, TGT_BLK, SLOTS)
    count_rep = tile_count.reshape(N_DP, TGT_BLK)
    values_rep = tile_values.reshape(N_DP, TGT_BLK, SLOTS, TILE, TILE)
    cot_rep = cotangent.reshape(N_DP, TGT_REP, HID_WIDTH)

    def replica(carry, items):
        feats, ids, index, count, values, cot = items
        blocks = feats.reshape(SRC_BLK, TILE, IN_WIDTH)
        picked = blocks[index]
        live_slot = jnp.arange(SLOTS, dtype=jnp.int32)[None, :] < count[:, None]
        masked = jnp.where(live_slot[:, :, None, None], values, jnp.zeros((), jnp.bfloat16))
        summed = jnp.einsum('bkij,bkjc->bic', masked.astype(jnp.float32), picked.astype(jnp.float32))
        aggregated = summed.reshape(TGT_REP, IN_WIDTH).astype(jnp.bfloat16)
        own_rows = feats[ids]
        preact = jnp.dot(aggregated, w_neigh, preferred_element_type=jnp.float32)
        preact = preact + jnp.dot(own_rows, w_self, preferred_element_type=jnp.float32) + bias
        output, pullback = jax.vjp(smooth, preact)
        grad_pre = pullback(cot.astype(jnp.float32))[0].astype(jnp.bfloat16)
        grad_n = lax.dot_general(aggregated, grad_pre, (((0,), (0,)), ((), ())), preferred_element_type=jnp.float32)
        grad_s = lax.dot_general(own_rows, grad_pre, (((0,), (0,)), ((), ())), preferred_element_type=jnp.float32)
        return ((carry[0] + grad_n, carry[1] + grad_s), output.astype(jnp.bfloat16))
    start_sums = (jnp.zeros((IN_WIDTH, HID_WIDTH), jnp.float32), jnp.zeros((IN_WIDTH, HID_WIDTH), jnp.float32))
    sums, outputs = lax.scan(replica, start_sums, (feat_rep, ids_rep, index_rep, count_rep, values_rep, cot_rep))
    return (outputs.reshape(TARGETS, HID_WIDTH), sums[0], sums[1])
```

```python
import jax
import jax.numpy as jnp
import numpy as np
from jax import lax
from jax.experimental import pallas as pl
from jax.experimental.pallas import tpu as pltpu
from jax.sharding import Mesh, PartitionSpec as P

TILE = 128
COLS = 48
NZ, NC, NY, NX = 8, 2, 4, 4
CHIP = 1024
HALF = 512
PIECE = 32
GATE = 0.7978845608028654
CUBE = 0.044715
BF, F32 = jnp.bfloat16, jnp.float32
VMEM = pl.BlockSpec(memory_space=pltpu.VMEM)
SMEM = pl.BlockSpec(memory_space=pltpu.SMEM)
ANY = pl.BlockSpec(memory_space=pl.ANY)


def params(mib=56):
    return pltpu.CompilerParams(vmem_limit_bytes=mib * 2**20)


def nt(left, right):
    return lax.dot_general(left, right, (((1,), (1,)), ((), ())), preferred_element_type=F32)


CUTS = 16
BLOCKS = 64


def aggregate_kernel(index_ref, count_ref, at_ref, feat_hbm, tiles_hbm, neigh_ref, self_ref, out_ref, feat, tiles, sems):
    per = BLOCKS // CUTS

    def tile_copy(i):
        cut = pl.ds(i * per, per)
        return pltpu.make_async_copy(tiles_hbm.at[cut], tiles.at[cut], sems.at[i])

    feat_copy = pltpu.make_async_copy(feat_hbm, feat, sems.at[CUTS])
    feat_copy.start()
    for i in range(CUTS):
        tile_copy(i).start()
    lanes = pl.ds(pl.multiple_of((at_ref[0] // 2) * TILE, TILE), TILE)
    odd = lax.rem(at_ref[0], 2) == 1
    pair = [ref[:, lanes].astype(F32) for ref in (neigh_ref, self_ref)]
    pair = [jnp.where(odd, v[:, 64:], v[:, :64]) for v in pair]
    weights = jnp.concatenate(pair, axis=1).astype(BF)
    for z in range(NZ):
        out_ref[z, :, CHIP:] = weights
    feat_copy.wait()

    def cut(i, _):
        tile_copy(i).wait()
        for blk in range(per):
            at = i * per + blk
            live = count_ref[at]
            sources, held = [], []
            for slot in range(4):
                start = pl.multiple_of(index_ref[at, slot] * TILE, TILE)
                part = feat[:, pl.ds(start, TILE)]
                sources.append(jnp.where(slot < live, part, jnp.zeros_like(part)))
                held.append(tiles[at, slot])
            total = nt(jnp.concatenate(sources, axis=1), jnp.concatenate(held, axis=1))
            lane = pl.multiple_of((lax.rem(i, CUTS // NZ) * per + blk) * TILE, TILE)
            out_ref[i // (CUTS // NZ), :, pl.ds(lane, TILE)] = total.astype(BF)
        return 0

    lax.fori_loop(0, CUTS, cut, 0)


def aggregate(feat_t, index, count, at, tiles, w_neigh, w_self):
    return pl.pallas_call(
        aggregate_kernel,
        in_specs=[SMEM, SMEM, SMEM, ANY, ANY, VMEM, VMEM],
        out_specs=VMEM,
        out_shape=jax.ShapeDtypeStruct((NZ, COLS, CHIP + TILE), BF),
        scratch_shapes=[
            pltpu.VMEM(feat_t.shape, BF),
            pltpu.VMEM(tiles.shape, BF),
            pltpu.SemaphoreType.DMA((CUTS + 1,)),
        ],
        compiler_params=params(),
        cost_estimate=pl.CostEstimate(flops=400_000_000, bytes_accessed=11_000_000, transcendentals=0),
        name="aggregate",
    )(index, count, at, feat_t, tiles, w_neigh, w_self)


def pick_kernel(core_ref, mine_ref, other_ref, neigh_ref, self_ref):
    width = NZ * COLS
    first = core_ref[0] == 0
    turned = [ref[...].reshape(width, TILE).astype(F32).T for ref in (mine_ref, other_ref)]
    for part, out in enumerate((neigh_ref, self_ref)):
        cut = [v[part * 64 : (part + 1) * 64] for v in turned]
        mine, other = [jnp.where(first, v[:PIECE], v[PIECE:]) for v in cut]
        out[:, :width] = jnp.where(first, mine, other).astype(BF)
        out[:, width:] = jnp.where(first, other, mine).astype(BF)


def pick_weights(core, mine, other):
    tail = pl.BlockSpec((NZ, COLS, TILE), lambda i: (0, 0, CHIP // TILE))
    shape = (PIECE, NC * NZ * COLS)
    return pl.pallas_call(
        pick_kernel,
        grid=(1,),
        in_specs=[SMEM, tail, tail],
        out_specs=[pl.BlockSpec(shape, lambda i: (0, 0))] * 2,
        out_shape=[jax.ShapeDtypeStruct(shape, BF)] * 2,
        compiler_params=params(),
        cost_estimate=pl.CostEstimate(flops=0, bytes_accessed=400_000, transcendentals=0),
        name="pick_weights",
    )(core, mine, other)


GROUP = 64


def own_kernel(ids_ref, feat_ref, *rest):
    out_ref, rows, picked = rest[-3:]
    wide = 512

    def spread(i, _):
        at = pl.multiple_of(i * wide, wide)
        rows[pl.ds(at, wide), 0:COLS] = feat_ref[:, pl.ds(at, wide)].astype(F32).T
        return 0

    lax.fori_loop(0, feat_ref.shape[1] // wide, spread, 0)

    def block(z, _):
        def group(g, _):
            base = g * GROUP
            for j in range(GROUP):
                picked[pl.ds(base + j, 1), :] = rows[pl.ds(ids_ref[z * CHIP + base + j], 1), :]
            return 0

        lax.fori_loop(0, CHIP // GROUP, group, 0)
        out_ref[z] = picked[:, 0:COLS].T.astype(BF)
        return 0

    lax.fori_loop(0, NZ, block, 0)


def own(feat_t, ids, after):
    return pl.pallas_call(
        own_kernel,
        in_specs=[SMEM, VMEM] + [ANY] * len(after),
        out_specs=VMEM,
        out_shape=jax.ShapeDtypeStruct((NZ, COLS, CHIP), BF),
        scratch_shapes=[pltpu.VMEM((feat_t.shape[1], TILE), F32), pltpu.VMEM((CHIP, TILE), F32)],
        compiler_params=params(),
        cost_estimate=pl.CostEstimate(flops=0, bytes_accessed=60_000_000, transcendentals=0),
        name="own_rows",
    )(ids, feat_t, *after)


def turn_kernel(core_ref, cot_ref, held_ref, mine_ref, other_ref, kept_ref):
    turned = cot_ref[...].astype(F32).T.astype(BF)
    low = jnp.concatenate([turned[0:32], turned[64:96]], axis=0)
    high = jnp.concatenate([turned[32:64], turned[96:128]], axis=0)
    first = core_ref[0] == 0
    mine_ref[...] = jnp.where(first, low, high)
    other_ref[...] = jnp.where(first, high, low)


def turn(core, cot, held):
    half = jax.ShapeDtypeStruct((HALF, HALF), BF)
    return pl.pallas_call(
        turn_kernel,
        grid=(8,),
        in_specs=[SMEM, pl.BlockSpec((HALF, TILE), lambda i: (0, i))] + [ANY],
        out_specs=[pl.BlockSpec((64, HALF), lambda i: (i, 0))] * 2 + [ANY],
        out_shape=[half, half, jax.ShapeDtypeStruct(held.shape, held.dtype)],
        input_output_aliases={2: 2},
        compiler_params=params(),
        cost_estimate=pl.CostEstimate(flops=0, bytes_accessed=4_000_000, transcendentals=0),
        name="turn_cotangent",
    )(core, cot, held)


def unturn_kernel(core_ref, mine_ref, other_ref, out_ref):
    first = core_ref[0] == 0
    low = jnp.where(first, mine_ref[...], other_ref[...])
    high = jnp.where(first, other_ref[...], mine_ref[...])
    both = jnp.concatenate([low[0:32], high[0:32], low[32:64], high[32:64]], axis=0)
    out_ref[...] = both.astype(F32).T.astype(BF)


def unturn(core, mine, other):
    return pl.pallas_call(
        unturn_kernel,
        grid=(8,),
        in_specs=[SMEM] + [pl.BlockSpec((64, HALF), lambda i: (i, 0))] * 2,
        out_specs=pl.BlockSpec((HALF, TILE), lambda i: (0, i)),
        out_shape=jax.ShapeDtypeStruct((HALF, 1024), BF),
        compiler_params=params(),
        cost_estimate=pl.CostEstimate(flops=0, bytes_accessed=4_000_000, transcendentals=0),
        name="unturn_activation",
    )(core, mine, other)


def hand_kernel(*refs):
    pass


def hand_on(value, after):
    return pl.pallas_call(
        hand_kernel,
        in_specs=[ANY] * (1 + len(after)),
        out_specs=ANY,
        out_shape=jax.ShapeDtypeStruct(value.shape, value.dtype),
        input_output_aliases={0: 0},
        compiler_params=params(16),
        cost_estimate=pl.CostEstimate(flops=0, bytes_accessed=0, transcendentals=0),
        name="hand_on",
    )(value, *after)


def layer_kernel(
    place_ref, agg_mine, agg_other, own_mine, own_other, n0, n1, n2, n3, s0, s1, s2, s3, bias_ref,
    cot_mine, cot_other, act_mine, act_other, grad_hbm, nodes, weights, cot, act, grads, in_sems, out_sems,
):
    core, x, y = place_ref[0], place_ref[1], place_ref[2]
    here = pl.ds(pl.multiple_of(core * HALF, HALF), HALF)
    there = pl.ds(pl.multiple_of((1 - core) * HALF, HALF), HALF)
    pairs = [
        (agg_mine.at[:, :, pl.ds(0, CHIP)], nodes.at[core]),
        (agg_other.at[:, :, pl.ds(0, CHIP)], nodes.at[1 - core]),
    ]
    for far, (over_xy, over_yx) in enumerate(zip((n0, n1, n2, n3), (s0, s1, s2, s3))):
        for near in range(4):
            for half, ref, sy, sx in ((0, over_xy, far, near), (1, over_yx, near, far)):
                block = lax.rem(y - sy + NY, NY) * NX + lax.rem(x - sx + NX, NX)
                pairs.append((ref.at[near], weights.at[block, :, pl.ds(half * 768, 768)]))
    pairs += [
        (own_mine, nodes.at[2 + core]),
        (own_other, nodes.at[3 - core]),
        (cot_mine, cot.at[:, here]),
        (cot_other, cot.at[:, there]),
    ]
    copies = [pltpu.make_async_copy(src, dst, in_sems.at[i]) for i, (src, dst) in enumerate(pairs)]
    for copy in copies:
        copy.start()
    for copy in copies:
        copy.wait()
    held = nodes[...].reshape(1536, CHIP)
    rows = HALF // 2
    sent = []

    def send(src, dst):
        sent.append(pltpu.make_async_copy(src, dst, out_sems.at[len(sent)]))
        sent[-1].start()

    for chunk in range(2):
        at = pl.ds(chunk * rows, rows)
        own_weights = weights[chunk * 8 : (chunk + 1) * 8].reshape(rows, 1536)
        v = jnp.dot(own_weights, held, preferred_element_type=F32) + bias_ref[at, :]
        sq = v * v
        t = jnp.tanh(GATE * (v + CUBE * (sq * v)))
        half = 0.5 * (1.0 + t)
        act[at, :] = (v * half).astype(BF)
        send(act.at[at, here], act_mine.at[at])
        send(act.at[at, there], act_other.at[at])
        slope = half + (0.5 * GATE) * v * (1.0 - t * t) * (1.0 + (3.0 * CUBE) * sq)
        grad = (cot[at, :].astype(F32) * slope).astype(BF)
        grads[at, :] = nt(grad, held).astype(BF)
        send(grads.at[at], grad_hbm.at[at])
    for copy in sent:
        copy.wait()


def layer(place, aggs, owns, weights, bias, cots):
    half = jax.ShapeDtypeStruct((HALF, HALF), BF)
    return pl.pallas_call(
        layer_kernel,
        in_specs=[SMEM] + [ANY] * 12 + [VMEM] + [ANY] * 2,
        out_specs=[ANY] * 3,
        out_shape=[half, half, jax.ShapeDtypeStruct((HALF, 1536), BF)],
        scratch_shapes=[
            pltpu.VMEM((4, NZ, COLS, CHIP), BF),
            pltpu.VMEM((16, PIECE, 1536), BF),
            pltpu.VMEM((HALF, CHIP), BF),
            pltpu.VMEM((HALF, CHIP), BF),
            pltpu.VMEM((HALF, 1536), BF),
            pltpu.SemaphoreType.DMA((38,)),
            pltpu.SemaphoreType.DMA((6,)),
        ],
        compiler_params=params(),
        cost_estimate=pl.CostEstimate(flops=3_200_000_000, bytes_accessed=9_000_000, transcendentals=524288),
        name="layer",
    )(place, *aggs, *owns, *weights, bias, *cots)


def stack_kernel(*refs):
    ins, outs, sems = refs[:8], refs[8:10], refs[10]
    copies = [pltpu.make_async_copy(ref, outs[i // 4].at[i % 4], sems.at[i]) for i, ref in enumerate(ins)]
    for copy in copies:
        copy.start()
    for copy in copies:
        copy.wait()


def stack_both(first, second):
    shape = jax.ShapeDtypeStruct((4, *first[0].shape), BF)
    return pl.pallas_call(
        stack_kernel,
        in_specs=[ANY] * 8,
        out_specs=[ANY] * 2,
        out_shape=[shape, shape],
        scratch_shapes=[pltpu.SemaphoreType.DMA((8,))],
        compiler_params=params(16),
        cost_estimate=pl.CostEstimate(flops=0, bytes_accessed=800_000, transcendentals=0),
        name="stack_both",
    )(*first, *second)


def add_kernel(in_hbm, after_ref, out_ref, held, sems):
    copies = [pltpu.make_async_copy(in_hbm.at[i], held.at[i], sems.at[i]) for i in range(16)]
    for copy in copies:
        copy.start()
    total = None
    for i, copy in enumerate(copies):
        copy.wait()
        term = held[i].astype(F32)
        total = term if total is None else total + term
    for z in range(NZ):
        for core in range(NC):
            cut = [total[:, ((part * NC + core) * NZ + z) * COLS :][:, :COLS] for part in range(2)]
            out_ref[z * NC + core] = jnp.concatenate(cut, axis=1).astype(BF)


def add_pieces(pieces, after):
    return pl.pallas_call(
        add_kernel,
        in_specs=[ANY, ANY],
        out_specs=VMEM,
        out_shape=jax.ShapeDtypeStruct((16, PIECE, 2 * COLS), BF),
        scratch_shapes=[pltpu.VMEM((16, PIECE, 1536), BF), pltpu.SemaphoreType.DMA((16,))],
        compiler_params=params(),
        cost_estimate=pl.CostEstimate(flops=800_000, bytes_accessed=1_700_000, transcendentals=0),
        name="add_pieces",
    )(pieces, after)


def last_kernel(in_ref, neigh_ref, self_ref):
    both = []
    for core in range(NC):
        total = in_ref[core].astype(F32)
        for z in range(1, NZ):
            total = total + in_ref[z * NC + core].astype(F32)
        both.append(total)
    turned = jnp.concatenate(both, axis=0).T
    neigh_ref[...] = turned[:COLS]
    self_ref[...] = turned[COLS:]


def add_last(pieces):
    shape = jax.ShapeDtypeStruct((COLS, 64), F32)
    return pl.pallas_call(
        last_kernel,
        in_specs=[VMEM],
        out_specs=[VMEM, VMEM],
        out_shape=[shape, shape],
        compiler_params=params(),
        cost_estimate=pl.CostEstimate(flops=50_000, bytes_accessed=200_000, transcendentals=0),
        name="add_last",
    )(pieces)


def swap(value):
    return lax.ppermute(value, "core", [(0, 1), (1, 0)])


def spread_ring(value, axis, size):
    return [value] + [
        lax.ppermute(value, axis, [(i, (i + s) % size) for i in range(size)]) for s in range(1, size)
    ]


def shards(features, target_ids, tile_index, tile_count, tile_values, w_neigh, w_self, bias, cotangent):
    core, x, y = lax.axis_index("core"), lax.axis_index("x"), lax.axis_index("y")
    dp = y * NX + x
    core_at = core.astype(jnp.int32).reshape(1)
    place = jnp.stack([core, x, y]).astype(jnp.int32)
    feat_t = features.T

    bias_here = lax.dynamic_index_in_dim(bias.reshape(16, NC, PIECE), core, 1, keepdims=False).reshape(HALF, 1)

    agg_sent = aggregate(
        feat_t, tile_index, tile_count, dp.astype(jnp.int32).reshape(1), tile_values, w_neigh, w_self
    )
    agg = lax.all_to_all(agg_sent, "z", 0, 0)
    own_sent = own(feat_t, target_ids, (agg_sent,))
    cot_mine, cot_other, own_sent = turn(core_at, cotangent, own_sent)
    own_rows = lax.all_to_all(own_sent, "z", 0, 0)

    agg = hand_on(agg, (own_sent,))
    agg_swapped = swap(agg)
    cot_swapped = swap(cot_other)
    w_n, w_s = pick_weights(core_at, agg, agg_swapped)
    n_x, s_y = stack_both(spread_ring(w_n, "x", NX), spread_ring(w_s, "y", NY))
    weights = spread_ring(n_x, "y", NY) + spread_ring(s_y, "x", NX)

    own_rows = hand_on(own_rows, (*weights, cot_swapped, bias_here, place))
    act_mine, act_other, grads = layer(
        place, (agg, agg_swapped), (own_rows, swap(own_rows)), weights, bias_here, (cot_mine, cot_swapped)
    )
    pieces = lax.all_to_all(grads.reshape(16, PIECE, 1536), ("y", "x"), 0, 0)
    activation = unturn(core_at, act_mine, swap(act_other))
    summed = add_pieces(pieces, activation)
    return activation, *add_last(lax.all_to_all(summed, ("z", "core"), 0, 0))


def solution(mesh):
    split = Mesh(mesh.devices.reshape(NY, NX, NZ, NC), ("y", "x", "z", "core"))
    dp, feat = ("y", "x"), ("z", "core")
    every = dp + feat
    placed = (
        P(dp, feat), P(dp), P(dp, None), P(dp), P(dp, None, None, None),
        P(feat, None), P(feat, None), P(), P(every, None),
    )
    return jax.shard_map(
        shards,
        mesh=split,
        in_specs=placed,
        out_specs=(P(every, None), P(feat, dp), P(feat, dp)),
        check_vma=False,
    )
```

```python
import jax
import jax.numpy as jnp
import numpy as np
from jax import lax
from jax.experimental import pallas as pl
from jax.experimental.pallas import tpu as pltpu
from jax.sharding import Mesh, PartitionSpec as P

TILE = 128
COLS = 48
NZ, NC, NY, NX = 8, 2, 4, 4
CHIP = 1024
HALF = 512
PIECE = 32
GATE = 0.7978845608028654
CUBE = 0.044715
BF, F32 = jnp.bfloat16, jnp.float32
VMEM = pl.BlockSpec(memory_space=pltpu.VMEM)
SMEM = pl.BlockSpec(memory_space=pltpu.SMEM)
ANY = pl.BlockSpec(memory_space=pl.ANY)
HBM = pl.BlockSpec(memory_space=pltpu.HBM)


def params(mib=56):
    return pltpu.CompilerParams(vmem_limit_bytes=mib * 2**20)


def nt(left, right):
    return lax.dot_general(left, right, (((1,), (1,)), ((), ())), preferred_element_type=F32)


CUTS = 8
BLOCKS = 64
WIDE = 256


def aggregate_kernel(index_ref, count_ref, feat_hbm, tiles_hbm, neigh_ref, self_ref, out_ref, feat, tiles, sems):
    per = BLOCKS // CUTS

    def tile_copy(i):
        cut = pl.ds(i * per, per)
        return pltpu.make_async_copy(tiles_hbm.at[cut], tiles.at[cut], sems.at[i])

    feat_copy = pltpu.make_async_copy(feat_hbm, feat, sems.at[CUTS])
    feat_copy.start()
    for i in range(CUTS):
        tile_copy(i).start()
    x, y = lax.axis_index("x"), lax.axis_index("y")
    weights = [neigh_ref[:, pl.ds(pl.multiple_of(y * WIDE, WIDE), WIDE)]]
    for far in range(NY):
        lanes = pl.ds(pl.multiple_of(far * WIDE + (x // 2) * TILE, TILE), TILE)
        both = self_ref[:, lanes].astype(F32)
        weights.append(jnp.where(lax.rem(x, 2) == 1, both[:, 64:], both[:, :64]).astype(BF))
    weights = jnp.concatenate(weights, axis=1)
    for z in range(NZ):
        out_ref[z, :, CHIP:] = weights
    feat_copy.wait()

    def cut(i, _):
        tile_copy(i).wait()
        for blk in range(per):
            at = i * per + blk
            live = count_ref[at]
            sources, held = [], []
            for slot in range(4):
                start = pl.multiple_of(index_ref[slot, at] * TILE, TILE)
                part = feat[:, pl.ds(start, TILE)]
                sources.append(jnp.where(slot < live, part, jnp.zeros_like(part)))
                held.append(tiles[at, slot])
            total = nt(jnp.concatenate(sources, axis=1), jnp.concatenate(held, axis=1))
            lane = pl.multiple_of((lax.rem(i, CUTS // NZ) * per + blk) * TILE, TILE)
            out_ref[i // (CUTS // NZ), :, pl.ds(lane, TILE)] = total.astype(BF)
        return 0

    lax.fori_loop(0, CUTS, cut, 0)


def aggregate(feat_t, index, count, tiles, w_neigh, w_self):
    return pl.pallas_call(
        aggregate_kernel,
        in_specs=[SMEM, SMEM, ANY, ANY, VMEM, VMEM],
        out_specs=VMEM,
        out_shape=jax.ShapeDtypeStruct((NZ, COLS, CHIP + 2 * WIDE), BF),
        scratch_shapes=[
            pltpu.VMEM(feat_t.shape, BF),
            pltpu.VMEM(tiles.shape, BF),
            pltpu.SemaphoreType.DMA((CUTS + 1,)),
        ],
        compiler_params=params(56),
        cost_estimate=pl.CostEstimate(flops=400_000_000, bytes_accessed=11_000_000, transcendentals=0),
        name="aggregate",
    )(index, count, feat_t, tiles, w_neigh, w_self)


def pick_kernel(core_ref, mine_ref, other_ref, neigh_ref, self_ref):
    width = NZ * COLS
    first = core_ref[0] == 0
    for part, out in enumerate((neigh_ref, self_ref)):
        lanes = slice(part * WIDE, (part + 1) * WIDE)
        turned = [ref[:, :, lanes].reshape(width, WIDE).astype(F32).T for ref in (mine_ref, other_ref)]
        for i in range(4):
            cut = [v[i * 64 : (i + 1) * 64] for v in turned]
            mine, other = [jnp.where(first, v[:PIECE], v[PIECE:]) for v in cut]
            out[i, :, :width] = jnp.where(first, mine, other).astype(BF)
            out[i, :, width:] = jnp.where(first, other, mine).astype(BF)


def pick_weights(core, mine, other):
    tail = pl.BlockSpec((NZ, COLS, 2 * WIDE), lambda i: (0, 0, CHIP // (2 * WIDE)))
    shape = (4, PIECE, NC * NZ * COLS)
    return pl.pallas_call(
        pick_kernel,
        grid=(1,),
        in_specs=[SMEM, tail, tail],
        out_specs=[pl.BlockSpec(shape, lambda i: (0, 0, 0))] * 2,
        out_shape=[jax.ShapeDtypeStruct(shape, BF)] * 2,
        compiler_params=params(16),
        cost_estimate=pl.CostEstimate(flops=0, bytes_accessed=1_600_000, transcendentals=0),
        name="pick_weights",
    )(core, mine, other)


GROUP = 64


def own_kernel(ids_ref, feat_ref, *rest):
    out_ref, rows, picked = rest[-3:]
    wide = 512

    def spread(i, _):
        at = pl.multiple_of(i * wide, wide)
        rows[pl.ds(at, wide), 0:COLS] = feat_ref[:, pl.ds(at, wide)].astype(F32).T
        return 0

    lax.fori_loop(0, feat_ref.shape[1] // wide, spread, 0)

    def block(z, _):
        def group(g, _):
            base = g * GROUP
            for j in range(GROUP):
                picked[pl.ds(base + j, 1), :] = rows[pl.ds(ids_ref[z * CHIP + base + j], 1), :]
            return 0

        lax.fori_loop(0, CHIP // GROUP, group, 0)
        out_ref[z] = picked[:, 0:COLS].T.astype(BF)
        return 0

    lax.fori_loop(0, NZ, block, 0)


def own(feat_t, ids, after):
    return pl.pallas_call(
        own_kernel,
        in_specs=[SMEM, VMEM] + [ANY] * len(after),
        out_specs=VMEM,
        out_shape=jax.ShapeDtypeStruct((NZ, COLS, CHIP), BF),
        scratch_shapes=[pltpu.VMEM((feat_t.shape[1], TILE), F32), pltpu.VMEM((CHIP, TILE), F32)],
        compiler_params=params(20),
        cost_estimate=pl.CostEstimate(flops=0, bytes_accessed=60_000_000, transcendentals=0),
        name="own_rows",
    )(ids, feat_t, *after)


def turn_kernel(core_ref, cot_ref, held_ref, mine_ref, other_ref, kept_ref):
    turned = cot_ref[...].astype(F32).T.astype(BF)
    low = jnp.concatenate([turned[0:32], turned[64:96]], axis=0)
    high = jnp.concatenate([turned[32:64], turned[96:128]], axis=0)
    first = core_ref[0] == 0
    mine_ref[...] = jnp.where(first, low, high)
    other_ref[...] = jnp.where(first, high, low)


def turn(core, cot, held):
    half = jax.ShapeDtypeStruct((HALF, HALF), BF)
    return pl.pallas_call(
        turn_kernel,
        grid=(8,),
        in_specs=[SMEM, pl.BlockSpec((HALF, TILE), lambda i: (0, i))] + [ANY],
        out_specs=[pl.BlockSpec((64, HALF), lambda i: (i, 0))] * 2 + [ANY],
        out_shape=[half, half, jax.ShapeDtypeStruct(held.shape, held.dtype)],
        input_output_aliases={2: 2},
        compiler_params=params(12),
        cost_estimate=pl.CostEstimate(flops=0, bytes_accessed=4_000_000, transcendentals=0),
        name="turn_cotangent",
    )(core, cot, held)


def unturn_kernel(core_ref, mine_ref, other_ref, out_ref, token_ref):
    first = core_ref[0] == 0
    low = jnp.where(first, mine_ref[...], other_ref[...])
    high = jnp.where(first, other_ref[...], mine_ref[...])
    both = jnp.concatenate([low[0:32], high[0:32], low[32:64], high[32:64]], axis=0)
    out_ref[...] = both.astype(F32).T.astype(BF)
    token_ref[...] = jnp.zeros_like(token_ref)


def unturn(core, mine, other):
    return pl.pallas_call(
        unturn_kernel,
        grid=(8,),
        in_specs=[SMEM] + [pl.BlockSpec((64, HALF), lambda i: (i, 0))] * 2,
        out_specs=[pl.BlockSpec((HALF, TILE), lambda i: (0, i)), pl.BlockSpec((8, TILE), lambda i: (0, 0))],
        out_shape=[jax.ShapeDtypeStruct((HALF, 1024), BF), jax.ShapeDtypeStruct((8, TILE), F32)],
        compiler_params=params(12),
        cost_estimate=pl.CostEstimate(flops=0, bytes_accessed=4_000_000, transcendentals=0),
        name="unturn_activation",
    )(core, mine, other)


def hand_kernel(*refs):
    pass


def hand_on(value, after):
    return pl.pallas_call(
        hand_kernel,
        in_specs=[HBM] * (1 + len(after)),
        out_specs=HBM,
        out_shape=jax.ShapeDtypeStruct(value.shape, value.dtype),
        input_output_aliases={0: 0},
        compiler_params=params(16),
        cost_estimate=pl.CostEstimate(flops=0, bytes_accessed=0, transcendentals=0),
        name="hand_on",
    )(value, *after)


def layer_kernel(
    place_ref, agg_mine, agg_other, own_mine, own_other, n0, n1, n2, n3, s0, s1, s2, s3, bias_ref,
    cot_mine, cot_other, act_mine, act_other, grad_hbm, nodes, weights, cot, act, grads, in_sems, out_sems,
):
    core, x, y = place_ref[0], place_ref[1], place_ref[2]
    here = pl.ds(pl.multiple_of(core * HALF, HALF), HALF)
    there = pl.ds(pl.multiple_of((1 - core) * HALF, HALF), HALF)
    pairs = [
        (agg_mine.at[:, :, pl.ds(0, CHIP)], nodes.at[core]),
        (agg_other.at[:, :, pl.ds(0, CHIP)], nodes.at[1 - core]),
    ]
    for far, (over_y, over_x) in enumerate(zip((n0, n1, n2, n3), (s0, s1, s2, s3))):
        for near in range(4):
            from_y, from_x = lax.rem(y - far + NY, NY) * NX + near, near * NX + lax.rem(x - far + NX, NX)
            for half, ref, block in ((0, over_y, from_y), (1, over_x, from_x)):
                pairs.append((ref.at[near], weights.at[block, :, pl.ds(half * 768, 768)]))
    pairs += [
        (own_mine, nodes.at[2 + core]),
        (own_other, nodes.at[3 - core]),
        (cot_mine, cot.at[:, here]),
        (cot_other, cot.at[:, there]),
    ]
    copies = [pltpu.make_async_copy(src, dst, in_sems.at[i]) for i, (src, dst) in enumerate(pairs)]
    for copy in copies:
        copy.start()
    for copy in copies:
        copy.wait()
    held = nodes[...].reshape(1536, CHIP)
    rows = HALF // 2
    sent = []

    def send(src, dst):
        sent.append(pltpu.make_async_copy(src, dst, out_sems.at[len(sent)]))
        sent[-1].start()

    for chunk in range(2):
        at = pl.ds(chunk * rows, rows)
        own_weights = weights[chunk * 8 : (chunk + 1) * 8].reshape(rows, 1536)
        v = jnp.dot(own_weights, held, preferred_element_type=F32) + bias_ref[at, :]
        sq = v * v
        t = jnp.tanh(GATE * (v + CUBE * (sq * v)))
        half = 0.5 * (1.0 + t)
        act[at, :] = (v * half).astype(BF)
        send(act.at[at, here], act_mine.at[at])
        send(act.at[at, there], act_other.at[at])
        slope = half + (0.5 * GATE) * v * (1.0 - t * t) * (1.0 + (3.0 * CUBE) * sq)
        grad = (cot[at, :].astype(F32) * slope).astype(BF)
        grads[chunk * 8 : (chunk + 1) * 8] = nt(grad, held).astype(BF).reshape(8, PIECE, 1536)
        for part in range(2):
            for side in range(NC):
                src = grads.at[pl.ds(chunk * 8, 8), :, pl.ds((part * NC + side) * 384, 384)]
                send(src, grad_hbm.at[pl.ds(chunk * 8, 8), side, :, pl.ds(part * 384, 384)])
    for copy in sent:
        copy.wait()


def layer(place, aggs, owns, weights, bias, cots):
    half = jax.ShapeDtypeStruct((HALF, HALF), BF)
    return pl.pallas_call(
        layer_kernel,
        in_specs=[SMEM] + [HBM] * 12 + [VMEM] + [HBM] * 2,
        out_specs=[HBM] * 3,
        out_shape=[half, half, jax.ShapeDtypeStruct((16, NC, PIECE, 768), BF)],
        scratch_shapes=[
            pltpu.VMEM((4, NZ, COLS, CHIP), BF),
            pltpu.VMEM((16, PIECE, 1536), BF),
            pltpu.VMEM((HALF, CHIP), BF),
            pltpu.VMEM((HALF, CHIP), BF),
            pltpu.VMEM((16, PIECE, 1536), BF),
            pltpu.SemaphoreType.DMA((38,)),
            pltpu.SemaphoreType.DMA((12,)),
        ],
        compiler_params=params(56),
        cost_estimate=pl.CostEstimate(flops=3_200_000_000, bytes_accessed=9_000_000, transcendentals=524288),
        name="layer",
    )(place, *aggs, *owns, *weights, bias, *cots)


def add_kernel(in_hbm, token_ref, out_ref, held, sems):
    copies = [pltpu.make_async_copy(in_hbm.at[i], held.at[i], sems.at[i]) for i in range(32)]
    for copy in copies:
        copy.start()
    totals = [None, None]
    for i, copy in enumerate(copies):
        copy.wait()
        term = held[i].astype(F32)
        totals[i % 2] = term if totals[i % 2] is None else totals[i % 2] + term
    total = jnp.concatenate(totals, axis=0)
    for z in range(NZ):
        cut = [total[:, (part * NZ + z) * COLS :][:, :COLS] for part in range(2)]
        out_ref[z] = jnp.concatenate(cut, axis=1).astype(BF)


def add_pieces(pieces, token):
    return pl.pallas_call(
        add_kernel,
        in_specs=[ANY, ANY],
        out_specs=VMEM,
        out_shape=jax.ShapeDtypeStruct((NZ, 64, 2 * COLS), BF),
        scratch_shapes=[pltpu.VMEM((32, PIECE, 768), BF), pltpu.SemaphoreType.DMA((32,))],
        compiler_params=params(8),
        cost_estimate=pl.CostEstimate(flops=800_000, bytes_accessed=1_700_000, transcendentals=0),
        name="add_pieces",
    )(pieces, token)


def last_kernel(in_ref, neigh_ref, self_ref):
    total = in_ref[0].astype(F32)
    for z in range(1, NZ):
        total = total + in_ref[z].astype(F32)
    turned = total.T
    neigh_ref[...] = turned[:COLS]
    self_ref[...] = turned[COLS:]


def add_last(pieces):
    shape = jax.ShapeDtypeStruct((COLS, 64), F32)
    return pl.pallas_call(
        last_kernel,
        in_specs=[VMEM],
        out_specs=[VMEM, VMEM],
        out_shape=[shape, shape],
        compiler_params=params(8),
        cost_estimate=pl.CostEstimate(flops=50_000, bytes_accessed=200_000, transcendentals=0),
        name="add_last",
    )(pieces)


def swap(value):
    return lax.ppermute(value, "core", [(0, 1), (1, 0)])


def spread_ring(value, axis, size):
    return [value] + [
        lax.ppermute(value, axis, [(i, (i + s) % size) for i in range(size)]) for s in range(1, size)
    ]


def shards(features, target_ids, tile_index, tile_count, tile_values, w_neigh, w_self, bias, cotangent):
    core, x, y = lax.axis_index("core"), lax.axis_index("x"), lax.axis_index("y")
    core_at = core.astype(jnp.int32).reshape(1)
    place = jnp.stack([core, x, y]).astype(jnp.int32)
    feat_t = features.T

    bias_here = lax.dynamic_index_in_dim(bias.reshape(16, NC, PIECE), core, 1, keepdims=False).reshape(HALF, 1)

    agg_sent = aggregate(
        feat_t, tile_index.T, tile_count, tile_values, w_neigh, w_self
    )
    agg = lax.all_to_all(agg_sent, "z", 0, 0)
    own_sent = own(feat_t, target_ids, (agg_sent,))
    cot_mine, cot_other, own_sent = turn(core_at, cotangent, own_sent)
    own_rows = lax.all_to_all(own_sent, "z", 0, 0)

    agg = hand_on(agg, (own_sent,))
    agg_swapped = swap(agg)
    cot_swapped = swap(cot_other)
    w_n, w_s = pick_weights(core_at, agg, agg_swapped)
    weights = spread_ring(w_n, "y", NY) + spread_ring(w_s, "x", NX)

    there = sum(w[0, :8, :TILE] for w in weights[1:4] + weights[5:]) + cot_swapped[:8, :TILE]
    own_rows = hand_on(own_rows, (there, bias_here, place))
    act_mine, act_other, grads = layer(
        place, (agg, agg_swapped), (own_rows, swap(own_rows)), weights, bias_here, (cot_mine, cot_swapped)
    )
    pieces = lax.all_to_all(grads.reshape(32, PIECE, 768), ("y", "x", "core"), 0, 0)
    activation, token = unturn(core_at, act_mine, swap(act_other))
    summed = add_pieces(pieces, token)
    return activation, *add_last(lax.all_to_all(summed, "z", 0, 0))


def solution(mesh):
    split = Mesh(mesh.devices.reshape(NY, NX, NZ, NC), ("y", "x", "z", "core"))
    dp, feat = ("y", "x"), ("z", "core")
    every = dp + feat
    placed = (
        P(dp, feat), P(dp), P(dp, None), P(dp), P(dp, None, None, None),
        P(feat, None), P(feat, None), P(), P(every, None),
    )
    return jax.shard_map(
        shards,
        mesh=split,
        in_specs=placed,
        out_specs=(P(every, None), P(feat, dp), P(feat, dp)),
        check_vma=False,
    )
```

```python
import functools

import jax
import jax.numpy as jnp
import numpy as np
from jax import lax
from jax.experimental import pallas as pl
from jax.experimental.pallas import tpu as pltpu
from jax.sharding import Mesh, PartitionSpec as P

TILE = 128
COLS = 48
NZ, NC, NY, NX = 8, 2, 4, 4
CHIP = 1024
HALF = 512
PIECE = 32
GATE = 0.7978845608028654
CUBE = 0.044715
BF, F32 = jnp.bfloat16, jnp.float32
VMEM = pl.BlockSpec(memory_space=pltpu.VMEM)
SMEM = pl.BlockSpec(memory_space=pltpu.SMEM)
ANY = pl.BlockSpec(memory_space=pl.ANY)
HBM = pl.BlockSpec(memory_space=pltpu.HBM)


def params(mib=56):
    return pltpu.CompilerParams(vmem_limit_bytes=mib * 2**20)


def nt(left, right):
    return lax.dot_general(left, right, (((1,), (1,)), ((), ())), preferred_element_type=F32)


WIDE = 256
PER = 4


def aggregate_kernel(half, index_ref, count_ref, feat_hbm, tiles_hbm, *rest):
    out_ref, feat, tiles, sems = rest[-4:]

    def tile_copy(z):
        src = tiles_hbm.at[pl.ds(z * 2 * PER + half * PER, PER)]
        return pltpu.make_async_copy(src, tiles.at[pl.ds(z * PER, PER)], sems.at[z])

    feat_copy = pltpu.make_async_copy(feat_hbm, feat, sems.at[NZ])
    feat_copy.start()
    for z in range(NZ):
        tile_copy(z).start()
    if half == 0:
        neigh_ref, self_ref = rest[:2]
        x, y = lax.axis_index("x"), lax.axis_index("y")
        weights = [neigh_ref[:, pl.ds(pl.multiple_of(y * WIDE, WIDE), WIDE)]]
        for far in range(NY):
            lanes = pl.ds(pl.multiple_of(far * WIDE + (x // 2) * TILE, TILE), TILE)
            both = self_ref[:, lanes].astype(F32)
            weights.append(jnp.where(lax.rem(x, 2) == 1, both[:, 64:], both[:, :64]).astype(BF))
        weights = jnp.concatenate(weights, axis=1)
        for z in range(NZ):
            out_ref[z, :, HALF:] = weights
    feat_copy.wait()

    def chip(z, _):
        tile_copy(z).wait()
        for blk in range(PER):
            at = z * 2 * PER + half * PER + blk
            live = count_ref[at]
            sources, held = [], []
            for slot in range(4):
                start = pl.multiple_of(index_ref[slot, at] * TILE, TILE)
                part = feat[:, pl.ds(start, TILE)]
                sources.append(jnp.where(slot < live, part, jnp.zeros_like(part)))
                held.append(tiles[z * PER + blk, slot])
            total = nt(jnp.concatenate(sources, axis=1), jnp.concatenate(held, axis=1))
            out_ref[z, :, blk * TILE : (blk + 1) * TILE] = total.astype(BF)
        return 0

    lax.fori_loop(0, NZ, chip, 0)


def aggregate(half, feat_t, index, count, tiles, extra):
    width = CHIP if half == 0 else HALF
    return pl.pallas_call(
        functools.partial(aggregate_kernel, half),
        in_specs=[SMEM, SMEM, ANY, ANY] + ([VMEM, VMEM] if half == 0 else [ANY]),
        out_specs=VMEM,
        out_shape=jax.ShapeDtypeStruct((NZ, COLS, width), BF),
        scratch_shapes=[
            pltpu.VMEM(feat_t.shape, BF),
            pltpu.VMEM((NZ * PER, *tiles.shape[1:]), BF),
            pltpu.SemaphoreType.DMA((NZ + 1,)),
        ],
        compiler_params=params(56),
        cost_estimate=pl.CostEstimate(flops=200_000_000, bytes_accessed=6_000_000, transcendentals=0),
        name="aggregate",
    )(index, count, feat_t, tiles, *extra)


def pick_kernel(core_ref, mine_ref, other_ref, neigh_ref, self_ref):
    width = NZ * COLS
    first = core_ref[0] == 0
    for part, out in enumerate((neigh_ref, self_ref)):
        lanes = slice(part * WIDE, (part + 1) * WIDE)
        turned = [ref[:, :, lanes].reshape(width, WIDE).astype(F32).T for ref in (mine_ref, other_ref)]
        for i in range(4):
            cut = [v[i * 64 : (i + 1) * 64] for v in turned]
            mine, other = [jnp.where(first, v[:PIECE], v[PIECE:]) for v in cut]
            out[i, :, :width] = jnp.where(first, mine, other).astype(BF)
            out[i, :, width:] = jnp.where(first, other, mine).astype(BF)


def pick_weights(core, mine, other):
    tail = pl.BlockSpec((NZ, COLS, 2 * WIDE), lambda i: (0, 0, 1))
    shape = (4, PIECE, NC * NZ * COLS)
    return pl.pallas_call(
        pick_kernel,
        grid=(1,),
        in_specs=[SMEM, tail, tail],
        out_specs=[pl.BlockSpec(shape, lambda i: (0, 0, 0))] * 2,
        out_shape=[jax.ShapeDtypeStruct(shape, BF)] * 2,
        compiler_params=params(16),
        cost_estimate=pl.CostEstimate(flops=0, bytes_accessed=1_600_000, transcendentals=0),
        name="pick_weights",
    )(core, mine, other)


GROUP = 128


def own_kernel(ids_ref, feat_ref, agg_ref, out_ref, rows, picked):
    out_ref[:, :, CHIP:] = agg_ref[...]
    wide = 512

    def spread(i, _):
        at = pl.multiple_of(i * wide, wide)
        rows[pl.ds(at, wide), 0:COLS] = feat_ref[:, pl.ds(at, wide)].astype(F32).T
        return 0

    lax.fori_loop(0, feat_ref.shape[1] // wide, spread, 0)

    def block(z, _):
        def group(g, _):
            base = g * GROUP
            for j in range(GROUP):
                picked[pl.ds(base + j, 1), :] = rows[pl.ds(ids_ref[z * CHIP + base + j], 1), :]
            return 0

        lax.fori_loop(0, CHIP // GROUP, group, 0)
        out_ref[z, :, :CHIP] = picked[:, 0:COLS].T.astype(BF)
        return 0

    lax.fori_loop(0, NZ, block, 0)


def own(feat_t, ids, agg):
    return pl.pallas_call(
        own_kernel,
        in_specs=[SMEM, VMEM, VMEM],
        out_specs=VMEM,
        out_shape=jax.ShapeDtypeStruct((NZ, COLS, CHIP + HALF), BF),
        scratch_shapes=[pltpu.VMEM((feat_t.shape[1], TILE), F32), pltpu.VMEM((CHIP, TILE), F32)],
        compiler_params=params(20),
        cost_estimate=pl.CostEstimate(flops=0, bytes_accessed=60_000_000, transcendentals=0),
        name="own_rows",
    )(ids, feat_t, agg)


def turn_kernel(core_ref, cot_ref, after_ref, mine_ref, other_ref):
    turned = cot_ref[...].astype(F32).T.astype(BF)
    low = jnp.concatenate([turned[0:32], turned[64:96]], axis=0)
    high = jnp.concatenate([turned[32:64], turned[96:128]], axis=0)
    first = core_ref[0] == 0
    mine_ref[...] = jnp.where(first, low, high)
    other_ref[...] = jnp.where(first, high, low)


def turn(core, cot, after):
    half = jax.ShapeDtypeStruct((HALF, HALF), BF)
    return pl.pallas_call(
        turn_kernel,
        grid=(8,),
        in_specs=[SMEM, pl.BlockSpec((HALF, TILE), lambda i: (0, i))] + [ANY],
        out_specs=[pl.BlockSpec((64, HALF), lambda i: (i, 0))] * 2,
        out_shape=[half, half],
        compiler_params=params(12),
        cost_estimate=pl.CostEstimate(flops=0, bytes_accessed=4_000_000, transcendentals=0),
        name="turn_cotangent",
    )(core, cot, after)


def unturn_kernel(core_ref, mine_ref, other_ref, out_ref, token_ref):
    first = core_ref[0] == 0
    low = jnp.where(first, mine_ref[...], other_ref[...])
    high = jnp.where(first, other_ref[...], mine_ref[...])
    both = jnp.concatenate([low[0:32], high[0:32], low[32:64], high[32:64]], axis=0)
    out_ref[...] = both.astype(F32).T.astype(BF)
    token_ref[...] = jnp.zeros_like(token_ref)


def unturn(core, mine, other):
    return pl.pallas_call(
        unturn_kernel,
        grid=(8,),
        in_specs=[SMEM] + [pl.BlockSpec((64, HALF), lambda i: (i, 0))] * 2,
        out_specs=[pl.BlockSpec((HALF, TILE), lambda i: (0, i)), pl.BlockSpec((8, TILE), lambda i: (0, 0))],
        out_shape=[jax.ShapeDtypeStruct((HALF, 1024), BF), jax.ShapeDtypeStruct((8, TILE), F32)],
        compiler_params=params(12),
        cost_estimate=pl.CostEstimate(flops=0, bytes_accessed=4_000_000, transcendentals=0),
        name="unturn_activation",
    )(core, mine, other)


def hand_kernel(*refs):
    pass


def hand_on(value, after):
    return pl.pallas_call(
        hand_kernel,
        in_specs=[HBM] * (1 + len(after)),
        out_specs=HBM,
        out_shape=jax.ShapeDtypeStruct(value.shape, value.dtype),
        input_output_aliases={0: 0},
        compiler_params=params(16),
        cost_estimate=pl.CostEstimate(flops=0, bytes_accessed=0, transcendentals=0),
        name="hand_on",
    )(value, *after)


def layer_kernel(
    place_ref, agg_mine, agg_other, own_mine, own_other, n0, n1, n2, n3, s0, s1, s2, s3, bias_ref,
    cot_mine, cot_other, act_mine, act_other, grad_hbm, nodes, weights, cot, act, grads, in_sems, out_sems,
):
    core, x, y = place_ref[0], place_ref[1], place_ref[2]
    here = pl.ds(pl.multiple_of(core * HALF, HALF), HALF)
    there = pl.ds(pl.multiple_of((1 - core) * HALF, HALF), HALF)
    pairs = []
    for first, second, at in ((agg_mine, own_mine, core), (agg_other, own_other, 1 - core)):
        pairs.append((first.at[:, :, pl.ds(0, HALF)], nodes.at[at, :, :, pl.ds(0, HALF)]))
        pairs.append((second.at[:, :, pl.ds(CHIP, HALF)], nodes.at[at, :, :, pl.ds(HALF, HALF)]))
        pairs.append((second.at[:, :, pl.ds(0, CHIP)], nodes.at[2 + at]))
    for far, (over_y, over_x) in enumerate(zip((n0, n1, n2, n3), (s0, s1, s2, s3))):
        for near in range(4):
            from_y, from_x = lax.rem(y - far + NY, NY) * NX + near, near * NX + lax.rem(x - far + NX, NX)
            for half, ref, block in ((0, over_y, from_y), (1, over_x, from_x)):
                pairs.append((ref.at[near], weights.at[block, :, pl.ds(half * 768, 768)]))
    pairs += [
        (cot_mine, cot.at[:, here]),
        (cot_other, cot.at[:, there]),
    ]
    copies = [pltpu.make_async_copy(src, dst, in_sems.at[i]) for i, (src, dst) in enumerate(pairs)]
    for copy in copies:
        copy.start()
    for copy in copies:
        copy.wait()
    held = nodes[...].reshape(1536, CHIP)
    rows = HALF // 2
    sent = []

    def send(src, dst):
        sent.append(pltpu.make_async_copy(src, dst, out_sems.at[len(sent)]))
        sent[-1].start()

    for chunk in range(2):
        at = pl.ds(chunk * rows, rows)
        own_weights = weights[chunk * 8 : (chunk + 1) * 8].reshape(rows, 1536)
        v = jnp.dot(own_weights, held, preferred_element_type=F32) + bias_ref[at, :]
        sq = v * v
        t = jnp.tanh(GATE * (v + CUBE * (sq * v)))
        half = 0.5 * (1.0 + t)
        act[at, :] = (v * half).astype(BF)
        send(act.at[at, here], act_mine.at[at])
        send(act.at[at, there], act_other.at[at])
        slope = half + (0.5 * GATE) * v * (1.0 - t * t) * (1.0 + (3.0 * CUBE) * sq)
        grad = (cot[at, :].astype(F32) * slope).astype(BF)
        grads[chunk * 8 : (chunk + 1) * 8] = nt(grad, held).astype(BF).reshape(8, PIECE, 1536)
        for part in range(2):
            for side in range(NC):
                src = grads.at[pl.ds(chunk * 8, 8), :, pl.ds((part * NC + side) * 384, 384)]
                send(src, grad_hbm.at[pl.ds(chunk * 8, 8), side, :, pl.ds(part * 384, 384)])
    for copy in sent:
        copy.wait()


def layer(place, aggs, owns, weights, bias, cots):
    half = jax.ShapeDtypeStruct((HALF, HALF), BF)
    return pl.pallas_call(
        layer_kernel,
        in_specs=[SMEM] + [HBM] * 12 + [VMEM] + [HBM] * 2,
        out_specs=[HBM] * 3,
        out_shape=[half, half, jax.ShapeDtypeStruct((16, NC, PIECE, 768), BF)],
        scratch_shapes=[
            pltpu.VMEM((4, NZ, COLS, CHIP), BF),
            pltpu.VMEM((16, PIECE, 1536), BF),
            pltpu.VMEM((HALF, CHIP), BF),
            pltpu.VMEM((HALF, CHIP), BF),
            pltpu.VMEM((16, PIECE, 1536), BF),
            pltpu.SemaphoreType.DMA((40,)),
            pltpu.SemaphoreType.DMA((12,)),
        ],
        compiler_params=params(56),
        cost_estimate=pl.CostEstimate(flops=3_200_000_000, bytes_accessed=9_000_000, transcendentals=524288),
        name="layer",
    )(place, *aggs, *owns, *weights, bias, *cots)


def add_kernel(in_hbm, token_ref, out_ref, held, sems):
    copies = [pltpu.make_async_copy(in_hbm.at[i], held.at[i], sems.at[i]) for i in range(32)]
    for copy in copies:
        copy.start()
    totals = [None, None]
    for i, copy in enumerate(copies):
        copy.wait()
        term = held[i].astype(F32)
        totals[i % 2] = term if totals[i % 2] is None else totals[i % 2] + term
    total = jnp.concatenate(totals, axis=0)
    for z in range(NZ):
        cut = [total[:, (part * NZ + z) * COLS :][:, :COLS] for part in range(2)]
        out_ref[z] = jnp.concatenate(cut, axis=1).astype(BF)


def add_pieces(pieces, token):
    return pl.pallas_call(
        add_kernel,
        in_specs=[ANY, ANY],
        out_specs=VMEM,
        out_shape=jax.ShapeDtypeStruct((NZ, 64, 2 * COLS), BF),
        scratch_shapes=[pltpu.VMEM((32, PIECE, 768), BF), pltpu.SemaphoreType.DMA((32,))],
        compiler_params=params(8),
        cost_estimate=pl.CostEstimate(flops=800_000, bytes_accessed=1_700_000, transcendentals=0),
        name="add_pieces",
    )(pieces, token)


def last_kernel(in_ref, neigh_ref, self_ref):
    total = in_ref[0].astype(F32)
    for z in range(1, NZ):
        total = total + in_ref[z].astype(F32)
    turned = total.T
    neigh_ref[...] = turned[:COLS]
    self_ref[...] = turned[COLS:]


def add_last(pieces):
    shape = jax.ShapeDtypeStruct((COLS, 64), F32)
    return pl.pallas_call(
        last_kernel,
        in_specs=[VMEM],
        out_specs=[VMEM, VMEM],
        out_shape=[shape, shape],
        compiler_params=params(8),
        cost_estimate=pl.CostEstimate(flops=50_000, bytes_accessed=200_000, transcendentals=0),
        name="add_last",
    )(pieces)


def swap(value):
    return lax.ppermute(value, "core", [(0, 1), (1, 0)])


def spread_ring(value, axis, size):
    return [value] + [
        lax.ppermute(value, axis, [(i, (i + s) % size) for i in range(size)]) for s in range(1, size)
    ]


def shards(features, target_ids, tile_index, tile_count, tile_values, w_neigh, w_self, bias, cotangent):
    core, x, y = lax.axis_index("core"), lax.axis_index("x"), lax.axis_index("y")
    core_at = core.astype(jnp.int32).reshape(1)
    place = jnp.stack([core, x, y]).astype(jnp.int32)
    feat_t = features.T

    bias_here = lax.dynamic_index_in_dim(bias.reshape(16, NC, PIECE), core, 1, keepdims=False).reshape(HALF, 1)

    agg_sent = aggregate(0, feat_t, tile_index.T, tile_count, tile_values, (w_neigh, w_self))
    agg = lax.all_to_all(agg_sent, "z", 0, 0)
    agg_late = aggregate(1, feat_t, tile_index.T, tile_count, tile_values, (agg_sent,))
    own_sent = own(feat_t, target_ids, agg_late)
    own_rows = lax.all_to_all(own_sent, "z", 0, 0)

    agg = hand_on(agg, (own_sent,))
    agg_swapped = swap(agg)
    w_n, w_s = pick_weights(core_at, agg, agg_swapped)
    cot_mine, cot_other = turn(core_at, cotangent, w_n)
    cot_swapped = swap(cot_other)
    weights = spread_ring(w_n, "y", NY) + spread_ring(w_s, "x", NX)

    there = sum(w[0, :8, :TILE] for w in weights[1:4] + weights[5:]) + cot_swapped[:8, :TILE]
    own_rows = hand_on(own_rows, (there, bias_here, place))
    act_mine, act_other, grads = layer(
        place, (agg, agg_swapped), (own_rows, swap(own_rows)), weights, bias_here, (cot_mine, cot_swapped)
    )
    pieces = lax.all_to_all(grads.reshape(32, PIECE, 768), ("y", "x", "core"), 0, 0)
    activation, token = unturn(core_at, act_mine, swap(act_other))
    summed = add_pieces(pieces, token)
    return activation, *add_last(lax.all_to_all(summed, "z", 0, 0))


def solution(mesh):
    split = Mesh(mesh.devices.reshape(NY, NX, NZ, NC), ("y", "x", "z", "core"))
    dp, feat = ("y", "x"), ("z", "core")
    every = dp + feat
    placed = (
        P(dp, feat), P(dp), P(dp, None), P(dp), P(dp, None, None, None),
        P(feat, None), P(feat, None), P(), P(every, None),
    )
    return jax.shard_map(
        shards,
        mesh=split,
        in_specs=placed,
        out_specs=(P(every, None), P(feat, dp), P(feat, dp)),
        check_vma=False,
    )
```

```python
import functools

import jax
import jax.numpy as jnp
import numpy as np
from jax import lax
from jax.experimental import pallas as pl
from jax.experimental.pallas import tpu as pltpu
from jax.sharding import Mesh, PartitionSpec as P

TILE = 128
COLS = 48
NZ, NC, NY, NX = 8, 2, 4, 4
CHIP = 1024
HALF = 512
PIECE = 32
GATE = 0.7978845608028654
CUBE = 0.044715
BF, F32 = jnp.bfloat16, jnp.float32
VMEM = pl.BlockSpec(memory_space=pltpu.VMEM)
SMEM = pl.BlockSpec(memory_space=pltpu.SMEM)
ANY = pl.BlockSpec(memory_space=pl.ANY)
HBM = pl.BlockSpec(memory_space=pltpu.HBM)


def params(mib=56):
    return pltpu.CompilerParams(vmem_limit_bytes=mib * 2**20)


def nt(left, right):
    return lax.dot_general(left, right, (((1,), (1,)), ((), ())), preferred_element_type=F32)


WIDE = 256
PER = 4


def aggregate_kernel(half, index_ref, count_ref, feat_hbm, tiles_hbm, *rest):
    out_ref, feat, tiles, sems = rest[-4:]

    def tile_copy(z):
        src = tiles_hbm.at[pl.ds(z * 2 * PER + half * PER, PER)]
        return pltpu.make_async_copy(src, tiles.at[pl.ds(z * PER, PER)], sems.at[z])

    feat_copy = pltpu.make_async_copy(feat_hbm, feat, sems.at[NZ])
    feat_copy.start()
    for z in range(NZ):
        tile_copy(z).start()
    if half == 0:
        neigh_ref, self_ref = rest[:2]
        x, y = lax.axis_index("x"), lax.axis_index("y")
        weights = [neigh_ref[:, pl.ds(pl.multiple_of(y * WIDE, WIDE), WIDE)]]
        for far in range(NY):
            lanes = pl.ds(pl.multiple_of(far * WIDE + (x // 2) * TILE, TILE), TILE)
            both = self_ref[:, lanes].astype(F32)
            weights.append(jnp.where(lax.rem(x, 2) == 1, both[:, 64:], both[:, :64]).astype(BF))
        weights = jnp.concatenate(weights, axis=1)
        for z in range(NZ):
            out_ref[z, :, HALF:] = weights
    feat_copy.wait()

    def chip(z, _):
        tile_copy(z).wait()
        for blk in range(PER):
            at = z * 2 * PER + half * PER + blk
            live = count_ref[at]
            sources, held = [], []
            for slot in range(4):
                start = pl.multiple_of(index_ref[slot, at] * TILE, TILE)
                part = feat[:, pl.ds(start, TILE)]
                sources.append(jnp.where(slot < live, part, jnp.zeros_like(part)))
                held.append(tiles[z * PER + blk, slot])
            total = nt(jnp.concatenate(sources, axis=1), jnp.concatenate(held, axis=1))
            out_ref[z, :, blk * TILE : (blk + 1) * TILE] = total.astype(BF)
        return 0

    lax.fori_loop(0, NZ, chip, 0)


def aggregate(half, feat_t, index, count, tiles, extra):
    width = CHIP if half == 0 else HALF
    return pl.pallas_call(
        functools.partial(aggregate_kernel, half),
        in_specs=[SMEM, SMEM, ANY, ANY] + ([VMEM, VMEM] if half == 0 else [ANY]),
        out_specs=VMEM,
        out_shape=jax.ShapeDtypeStruct((NZ, COLS, width), BF),
        scratch_shapes=[
            pltpu.VMEM(feat_t.shape, BF),
            pltpu.VMEM((NZ * PER, *tiles.shape[1:]), BF),
            pltpu.SemaphoreType.DMA((NZ + 1,)),
        ],
        compiler_params=params(56),
        cost_estimate=pl.CostEstimate(flops=200_000_000, bytes_accessed=6_000_000, transcendentals=0),
        name="aggregate",
    )(index, count, feat_t, tiles, *extra)


def pick_kernel(core_ref, mine_ref, other_ref, neigh_ref, self_ref):
    width = NZ * COLS
    first = core_ref[0] == 0
    for part, out in enumerate((neigh_ref, self_ref)):
        lanes = slice(part * WIDE, (part + 1) * WIDE)
        turned = [ref[:, :, lanes].reshape(width, WIDE).astype(F32).T for ref in (mine_ref, other_ref)]
        for i in range(4):
            cut = [v[i * 64 : (i + 1) * 64] for v in turned]
            mine, other = [jnp.where(first, v[:PIECE], v[PIECE:]) for v in cut]
            out[i, :, :width] = jnp.where(first, mine, other).astype(BF)
            out[i, :, width:] = jnp.where(first, other, mine).astype(BF)


def pick_weights(core, mine, other):
    tail = pl.BlockSpec((NZ, COLS, 2 * WIDE), lambda i: (0, 0, 1))
    shape = (4, PIECE, NC * NZ * COLS)
    return pl.pallas_call(
        pick_kernel,
        grid=(1,),
        in_specs=[SMEM, tail, tail],
        out_specs=[pl.BlockSpec(shape, lambda i: (0, 0, 0))] * 2,
        out_shape=[jax.ShapeDtypeStruct(shape, BF)] * 2,
        compiler_params=params(16),
        cost_estimate=pl.CostEstimate(flops=0, bytes_accessed=1_600_000, transcendentals=0),
        name="pick_weights",
    )(core, mine, other)


GROUP = 128


def own_kernel(ids_ref, feat_ref, agg_ref, out_ref, rows, picked):
    out_ref[:, :, CHIP:] = agg_ref[...]
    wide = 512

    def spread(i, _):
        at = pl.multiple_of(i * wide, wide)
        rows[pl.ds(at, wide), 0:COLS] = feat_ref[:, pl.ds(at, wide)].astype(F32).T
        return 0

    lax.fori_loop(0, feat_ref.shape[1] // wide, spread, 0)

    def block(z, _):
        def group(g, _):
            base = g * GROUP
            for j in range(GROUP):
                picked[pl.ds(base + j, 1), :] = rows[pl.ds(ids_ref[z * CHIP + base + j], 1), :]
            return 0

        lax.fori_loop(0, CHIP // GROUP, group, 0)
        out_ref[z, :, :CHIP] = picked[:, 0:COLS].T.astype(BF)
        return 0

    lax.fori_loop(0, NZ, block, 0)


def own(feat_t, ids, agg):
    return pl.pallas_call(
        own_kernel,
        in_specs=[SMEM, VMEM, VMEM],
        out_specs=VMEM,
        out_shape=jax.ShapeDtypeStruct((NZ, COLS, CHIP + HALF), BF),
        scratch_shapes=[pltpu.VMEM((feat_t.shape[1], TILE), F32), pltpu.VMEM((CHIP, TILE), F32)],
        compiler_params=params(20),
        cost_estimate=pl.CostEstimate(flops=0, bytes_accessed=60_000_000, transcendentals=0),
        name="own_rows",
    )(ids, feat_t, agg)


def turn_kernel(core_ref, cot_ref, after_ref, mine_ref, other_ref):
    turned = cot_ref[...].astype(F32).T.astype(BF)
    low = jnp.concatenate([turned[0:32], turned[64:96]], axis=0)
    high = jnp.concatenate([turned[32:64], turned[96:128]], axis=0)
    first = core_ref[0] == 0
    mine_ref[...] = jnp.where(first, low, high)
    other_ref[...] = jnp.where(first, high, low)


def turn(core, cot, after):
    half = jax.ShapeDtypeStruct((HALF, HALF), BF)
    return pl.pallas_call(
        turn_kernel,
        grid=(8,),
        in_specs=[SMEM, pl.BlockSpec((HALF, TILE), lambda i: (0, i))] + [ANY],
        out_specs=[pl.BlockSpec((64, HALF), lambda i: (i, 0))] * 2,
        out_shape=[half, half],
        compiler_params=params(12),
        cost_estimate=pl.CostEstimate(flops=0, bytes_accessed=4_000_000, transcendentals=0),
        name="turn_cotangent",
    )(core, cot, after)


def unturn_kernel(core_ref, mine_ref, other_ref, out_ref, token_ref):
    first = core_ref[0] == 0
    low = jnp.where(first, mine_ref[...], other_ref[...])
    high = jnp.where(first, other_ref[...], mine_ref[...])
    both = jnp.concatenate([low[0:32], high[0:32], low[32:64], high[32:64]], axis=0)
    out_ref[...] = both.astype(F32).T.astype(BF)
    token_ref[...] = jnp.zeros_like(token_ref)


def unturn(core, mine, other):
    return pl.pallas_call(
        unturn_kernel,
        grid=(8,),
        in_specs=[SMEM] + [pl.BlockSpec((64, HALF), lambda i: (i, 0))] * 2,
        out_specs=[pl.BlockSpec((HALF, TILE), lambda i: (0, i)), pl.BlockSpec((8, TILE), lambda i: (0, 0))],
        out_shape=[jax.ShapeDtypeStruct((HALF, 1024), BF), jax.ShapeDtypeStruct((8, TILE), F32)],
        compiler_params=params(12),
        cost_estimate=pl.CostEstimate(flops=0, bytes_accessed=4_000_000, transcendentals=0),
        name="unturn_activation",
    )(core, mine, other)


def hand_kernel(*refs):
    pass


def hand_on(value, after):
    return pl.pallas_call(
        hand_kernel,
        in_specs=[HBM] * (1 + len(after)),
        out_specs=HBM,
        out_shape=jax.ShapeDtypeStruct(value.shape, value.dtype),
        input_output_aliases={0: 0},
        compiler_params=params(16),
        cost_estimate=pl.CostEstimate(flops=0, bytes_accessed=0, transcendentals=0),
        name="hand_on",
    )(value, *after)


def layer_kernel(
    place_ref, agg_mine, agg_other, own_mine, own_other, n0, n1, n2, n3, s0, s1, s2, s3, bias_ref,
    cot_mine, cot_other, act_mine, act_other, grad_hbm, nodes, weights, cot, act, grads, in_sems, out_sems,
):
    core, x, y = place_ref[0], place_ref[1], place_ref[2]
    here = pl.ds(pl.multiple_of(core * HALF, HALF), HALF)
    there = pl.ds(pl.multiple_of((1 - core) * HALF, HALF), HALF)
    pairs = []
    for first, second, at in ((agg_mine, own_mine, core), (agg_other, own_other, 1 - core)):
        pairs.append((first.at[:, :, pl.ds(0, HALF)], nodes.at[at, :, :, pl.ds(0, HALF)]))
        pairs.append((second.at[:, :, pl.ds(CHIP, HALF)], nodes.at[at, :, :, pl.ds(HALF, HALF)]))
        pairs.append((second.at[:, :, pl.ds(0, CHIP)], nodes.at[2 + at]))
    for far, (over_y, over_x) in enumerate(zip((n0, n1, n2, n3), (s0, s1, s2, s3))):
        for near in range(4):
            from_y, from_x = lax.rem(y - far + NY, NY) * NX + near, near * NX + lax.rem(x - far + NX, NX)
            for half, ref, block in ((0, over_y, from_y), (1, over_x, from_x)):
                pairs.append((ref.at[near], weights.at[block, :, pl.ds(half * 768, 768)]))
    pairs += [
        (cot_mine, cot.at[:, here]),
        (cot_other, cot.at[:, there]),
    ]
    copies = [pltpu.make_async_copy(src, dst, in_sems.at[i]) for i, (src, dst) in enumerate(pairs)]
    for copy in copies:
        copy.start()
    for copy in copies:
        copy.wait()
    held = nodes[...].reshape(1536, CHIP)
    rows = HALF // 2
    sent = []

    def send(src, dst):
        sent.append(pltpu.make_async_copy(src, dst, out_sems.at[len(sent)]))
        sent[-1].start()

    for chunk in range(2):
        at = pl.ds(chunk * rows, rows)
        own_weights = weights[chunk * 8 : (chunk + 1) * 8].reshape(rows, 1536)
        v = jnp.dot(own_weights, held, preferred_element_type=F32) + bias_ref[at, :]
        sq = v * v
        t = jnp.tanh(GATE * (v + CUBE * (sq * v)))
        half = 0.5 * (1.0 + t)
        act[at, :] = (v * half).astype(BF)
        send(act.at[at, here], act_mine.at[at])
        send(act.at[at, there], act_other.at[at])
        slope = half + (0.5 * GATE) * v * (1.0 - t * t) * (1.0 + (3.0 * CUBE) * sq)
        grad = (cot[at, :].astype(F32) * slope).astype(BF)
        grads[chunk * 8 : (chunk + 1) * 8] = nt(grad, held).astype(BF).reshape(8, PIECE, 1536)
        for part in range(2):
            for side in range(NC):
                src = grads.at[pl.ds(chunk * 8, 8), :, pl.ds((part * NC + side) * 384, 384)]
                send(src, grad_hbm.at[pl.ds(chunk * 8, 8), side, :, pl.ds(part * 384, 384)])
    for copy in sent:
        copy.wait()


def layer(place, aggs, owns, weights, bias, cots):
    half = jax.ShapeDtypeStruct((HALF, HALF), BF)
    return pl.pallas_call(
        layer_kernel,
        in_specs=[SMEM] + [HBM] * 12 + [VMEM] + [HBM] * 2,
        out_specs=[HBM] * 3,
        out_shape=[half, half, jax.ShapeDtypeStruct((16, NC, PIECE, 768), BF)],
        scratch_shapes=[
            pltpu.VMEM((4, NZ, COLS, CHIP), BF),
            pltpu.VMEM((16, PIECE, 1536), BF),
            pltpu.VMEM((HALF, CHIP), BF),
            pltpu.VMEM((HALF, CHIP), BF),
            pltpu.VMEM((16, PIECE, 1536), BF),
            pltpu.SemaphoreType.DMA((40,)),
            pltpu.SemaphoreType.DMA((12,)),
        ],
        compiler_params=params(56),
        cost_estimate=pl.CostEstimate(flops=3_200_000_000, bytes_accessed=9_000_000, transcendentals=524288),
        name="layer",
    )(place, *aggs, *owns, *weights, bias, *cots)


def add_kernel(in_hbm, token_ref, out_ref, held, sems):
    copies = [pltpu.make_async_copy(in_hbm.at[i], held.at[i], sems.at[i]) for i in range(32)]
    for copy in copies:
        copy.start()
    totals = [None, None]
    for i, copy in enumerate(copies):
        copy.wait()
        term = held[i].astype(F32)
        totals[i % 2] = term if totals[i % 2] is None else totals[i % 2] + term
    total = jnp.concatenate(totals, axis=0)
    for z in range(NZ):
        cut = [total[:, (part * NZ + z) * COLS :][:, :COLS] for part in range(2)]
        out_ref[z] = jnp.concatenate(cut, axis=1).astype(BF)


def add_pieces(pieces, token):
    return pl.pallas_call(
        add_kernel,
        in_specs=[ANY, ANY],
        out_specs=VMEM,
        out_shape=jax.ShapeDtypeStruct((NZ, 64, 2 * COLS), BF),
        scratch_shapes=[pltpu.VMEM((32, PIECE, 768), BF), pltpu.SemaphoreType.DMA((32,))],
        compiler_params=params(8),
        cost_estimate=pl.CostEstimate(flops=800_000, bytes_accessed=1_700_000, transcendentals=0),
        name="add_pieces",
    )(pieces, token)


def last_kernel(in_ref, neigh_ref, self_ref):
    total = in_ref[0].astype(F32)
    for z in range(1, NZ):
        total = total + in_ref[z].astype(F32)
    turned = total.T
    neigh_ref[...] = turned[:COLS]
    self_ref[...] = turned[COLS:]


def add_last(pieces):
    shape = jax.ShapeDtypeStruct((COLS, 64), F32)
    return pl.pallas_call(
        last_kernel,
        in_specs=[VMEM],
        out_specs=[VMEM, VMEM],
        out_shape=[shape, shape],
        compiler_params=params(8),
        cost_estimate=pl.CostEstimate(flops=50_000, bytes_accessed=200_000, transcendentals=0),
        name="add_last",
    )(pieces)


def swap(value):
    return lax.ppermute(value, "core", [(0, 1), (1, 0)])


def spread_ring(value, axis, size):
    return [value] + [
        lax.ppermute(value, axis, [(i, (i + s) % size) for i in range(size)]) for s in range(1, size)
    ]


def shards(features, target_ids, tile_index, tile_count, tile_values, w_neigh, w_self, bias, cotangent):
    core, x, y = lax.axis_index("core"), lax.axis_index("x"), lax.axis_index("y")
    core_at = core.astype(jnp.int32).reshape(1)
    place = jnp.stack([core, x, y]).astype(jnp.int32)
    feat_t = features.T

    bias_here = lax.dynamic_index_in_dim(bias.reshape(16, NC, PIECE), core, 1, keepdims=False).reshape(HALF, 1)

    agg_sent = aggregate(0, feat_t, tile_index.T, tile_count, tile_values, (w_neigh, w_self))
    agg = lax.all_to_all(agg_sent, "z", 0, 0)
    agg_late = aggregate(1, feat_t, tile_index.T, tile_count, tile_values, (agg_sent,))
    own_sent = own(feat_t, target_ids, agg_late)
    own_rows = lax.all_to_all(own_sent, "z", 0, 0)

    agg = hand_on(agg, (own_sent,))
    agg_swapped = swap(agg)
    w_n, w_s = pick_weights(core_at, agg, agg_swapped)
    weights = spread_ring(w_n, "y", NY) + spread_ring(w_s, "x", NX)

    there = sum(w[0, :8, :TILE] for w in weights[1:4] + weights[5:])
    cot_mine, cot_other = turn(core_at, cotangent, there)
    cot_swapped = swap(cot_other)
    own_rows = hand_on(own_rows, (there + cot_other[:8, :TILE], bias_here, place))
    act_mine, act_other, grads = layer(
        place, (agg, agg_swapped), (own_rows, swap(own_rows)), weights, bias_here, (cot_mine, cot_swapped)
    )
    pieces = lax.all_to_all(grads.reshape(32, PIECE, 768), ("y", "x", "core"), 0, 0)
    activation, token = unturn(core_at, act_mine, swap(act_other))
    summed = add_pieces(pieces, token)
    return activation, *add_last(lax.all_to_all(summed, "z", 0, 0))


def solution(mesh):
    split = Mesh(mesh.devices.reshape(NY, NX, NZ, NC), ("y", "x", "z", "core"))
    dp, feat = ("y", "x"), ("z", "core")
    every = dp + feat
    placed = (
        P(dp, feat), P(dp), P(dp, None), P(dp), P(dp, None, None, None),
        P(feat, None), P(feat, None), P(), P(every, None),
    )
    return jax.shard_map(
        shards,
        mesh=split,
        in_specs=placed,
        out_specs=(P(every, None), P(feat, dp), P(feat, dp)),
        check_vma=False,
    )
```

```python
import functools

import jax
import jax.numpy as jnp
import numpy as np
from jax import lax
from jax.experimental import pallas as pl
from jax.experimental.pallas import tpu as pltpu
from jax.sharding import Mesh, PartitionSpec as P

TILE = 128
COLS = 48
NZ, NC, NY, NX = 8, 2, 4, 4
CHIP = 1024
HALF = 512
PIECE = 32
GATE = 0.7978845608028654
CUBE = 0.044715
BF, F32 = jnp.bfloat16, jnp.float32
VMEM = pl.BlockSpec(memory_space=pltpu.VMEM)
SMEM = pl.BlockSpec(memory_space=pltpu.SMEM)
ANY = pl.BlockSpec(memory_space=pl.ANY)
HBM = pl.BlockSpec(memory_space=pltpu.HBM)


def params(mib=56):
    return pltpu.CompilerParams(vmem_limit_bytes=mib * 2**20)


def nt(left, right):
    return lax.dot_general(left, right, (((1,), (1,)), ((), ())), preferred_element_type=F32)


WIDE = 256
PER = 4


def aggregate_kernel(half, index_ref, count_ref, feat_hbm, tiles_hbm, *rest):
    out_ref, feat, tiles, sems = rest[-4:]

    def tile_copy(z):
        src = tiles_hbm.at[pl.ds(z * 2 * PER + half * PER, PER)]
        return pltpu.make_async_copy(src, tiles.at[pl.ds(z * PER, PER)], sems.at[z])

    feat_copy = pltpu.make_async_copy(feat_hbm, feat, sems.at[NZ])
    feat_copy.start()
    for z in range(NZ):
        tile_copy(z).start()
    if half == 0:
        neigh_ref, self_ref = rest[:2]
        x, y = lax.axis_index("x"), lax.axis_index("y")
        weights = [neigh_ref[:, pl.ds(pl.multiple_of(y * WIDE, WIDE), WIDE)]]
        for far in range(NY):
            lanes = pl.ds(pl.multiple_of(far * WIDE + (x // 2) * TILE, TILE), TILE)
            both = self_ref[:, lanes].astype(F32)
            weights.append(jnp.where(lax.rem(x, 2) == 1, both[:, 64:], both[:, :64]).astype(BF))
        weights = jnp.concatenate(weights, axis=1)
        for z in range(NZ):
            out_ref[z, :, HALF:] = weights
    feat_copy.wait()

    def chip(z, _):
        tile_copy(z).wait()
        for blk in range(PER):
            at = z * 2 * PER + half * PER + blk
            live = count_ref[at]
            sources, held = [], []
            for slot in range(4):
                start = pl.multiple_of(index_ref[slot, at] * TILE, TILE)
                part = feat[:, pl.ds(start, TILE)]
                sources.append(jnp.where(slot < live, part, jnp.zeros_like(part)))
                held.append(tiles[z * PER + blk, slot])
            total = nt(jnp.concatenate(sources, axis=1), jnp.concatenate(held, axis=1))
            out_ref[z, :, blk * TILE : (blk + 1) * TILE] = total.astype(BF)
        return 0

    lax.fori_loop(0, NZ, chip, 0)


def aggregate(half, feat_t, index, count, tiles, extra):
    width = CHIP if half == 0 else HALF
    return pl.pallas_call(
        functools.partial(aggregate_kernel, half),
        in_specs=[SMEM, SMEM, ANY, ANY] + ([VMEM, VMEM] if half == 0 else [ANY]),
        out_specs=VMEM,
        out_shape=jax.ShapeDtypeStruct((NZ, COLS, width), BF),
        scratch_shapes=[
            pltpu.VMEM(feat_t.shape, BF),
            pltpu.VMEM((NZ * PER, *tiles.shape[1:]), BF),
            pltpu.SemaphoreType.DMA((NZ + 1,)),
        ],
        compiler_params=params(56),
        cost_estimate=pl.CostEstimate(flops=200_000_000, bytes_accessed=6_000_000, transcendentals=0),
        name="aggregate",
    )(index, count, feat_t, tiles, *extra)


def pick_kernel(core_ref, mine_ref, other_ref, neigh_ref, self_ref):
    width = NZ * COLS
    first = core_ref[0] == 0
    for part, out in enumerate((neigh_ref, self_ref)):
        lanes = slice(part * WIDE, (part + 1) * WIDE)
        turned = [ref[:, :, lanes].reshape(width, WIDE).astype(F32).T for ref in (mine_ref, other_ref)]
        for i in range(4):
            cut = [v[i * 64 : (i + 1) * 64] for v in turned]
            mine, other = [jnp.where(first, v[:PIECE], v[PIECE:]) for v in cut]
            out[i, :, :width] = jnp.where(first, mine, other).astype(BF)
            out[i, :, width:] = jnp.where(first, other, mine).astype(BF)


def pick_weights(core, mine, other):
    tail = pl.BlockSpec((NZ, COLS, 2 * WIDE), lambda i: (0, 0, 1))
    shape = (4, PIECE, NC * NZ * COLS)
    return pl.pallas_call(
        pick_kernel,
        grid=(1,),
        in_specs=[SMEM, tail, tail],
        out_specs=[pl.BlockSpec(shape, lambda i: (0, 0, 0))] * 2,
        out_shape=[jax.ShapeDtypeStruct(shape, BF)] * 2,
        compiler_params=params(16),
        cost_estimate=pl.CostEstimate(flops=0, bytes_accessed=1_600_000, transcendentals=0),
        name="pick_weights",
    )(core, mine, other)


GROUP = 128


def own_kernel(ids_ref, feat_ref, agg_ref, out_ref, rows, picked):
    out_ref[:, :, CHIP:] = agg_ref[...]
    wide = 512

    def spread(i, _):
        at = pl.multiple_of(i * wide, wide)
        rows[pl.ds(at, wide), 0:COLS] = feat_ref[:, pl.ds(at, wide)].astype(F32).T
        return 0

    lax.fori_loop(0, feat_ref.shape[1] // wide, spread, 0)

    def block(z, _):
        def group(g, _):
            base = g * GROUP
            for j in range(GROUP):
                picked[pl.ds(base + j, 1), :] = rows[pl.ds(ids_ref[z * CHIP + base + j], 1), :]
            return 0

        lax.fori_loop(0, CHIP // GROUP, group, 0)
        out_ref[z, :, :CHIP] = picked[:, 0:COLS].T.astype(BF)
        return 0

    lax.fori_loop(0, NZ, block, 0)


def own(feat_t, ids, agg):
    return pl.pallas_call(
        own_kernel,
        in_specs=[SMEM, VMEM, VMEM],
        out_specs=VMEM,
        out_shape=jax.ShapeDtypeStruct((NZ, COLS, CHIP + HALF), BF),
        scratch_shapes=[pltpu.VMEM((feat_t.shape[1], TILE), F32), pltpu.VMEM((CHIP, TILE), F32)],
        compiler_params=params(20),
        cost_estimate=pl.CostEstimate(flops=0, bytes_accessed=60_000_000, transcendentals=0),
        name="own_rows",
    )(ids, feat_t, agg)


def turn_kernel(core_ref, cot_ref, after_ref, mine_ref, other_ref):
    turned = cot_ref[...].astype(F32).T.astype(BF)
    low = jnp.concatenate([turned[0:32], turned[64:96]], axis=0)
    high = jnp.concatenate([turned[32:64], turned[96:128]], axis=0)
    first = core_ref[0] == 0
    mine_ref[...] = jnp.where(first, low, high)
    other_ref[...] = jnp.where(first, high, low)


def turn(core, cot, after):
    half = jax.ShapeDtypeStruct((HALF, HALF), BF)
    return pl.pallas_call(
        turn_kernel,
        grid=(8,),
        in_specs=[SMEM, pl.BlockSpec((HALF, TILE), lambda i: (0, i))] + [ANY],
        out_specs=[pl.BlockSpec((64, HALF), lambda i: (i, 0))] * 2,
        out_shape=[half, half],
        compiler_params=params(12),
        cost_estimate=pl.CostEstimate(flops=0, bytes_accessed=4_000_000, transcendentals=0),
        name="turn_cotangent",
    )(core, cot, after)


def unturn_kernel(core_ref, mine_ref, other_ref, out_ref, token_ref):
    first = core_ref[0] == 0
    low = jnp.where(first, mine_ref[...], other_ref[...])
    high = jnp.where(first, other_ref[...], mine_ref[...])
    both = jnp.concatenate([low[0:32], high[0:32], low[32:64], high[32:64]], axis=0)
    out_ref[...] = both.astype(F32).T.astype(BF)
    token_ref[...] = jnp.zeros_like(token_ref)


def unturn(core, mine, other):
    return pl.pallas_call(
        unturn_kernel,
        grid=(8,),
        in_specs=[SMEM] + [pl.BlockSpec((64, HALF), lambda i: (i, 0))] * 2,
        out_specs=[pl.BlockSpec((HALF, TILE), lambda i: (0, i)), pl.BlockSpec((8, TILE), lambda i: (0, 0))],
        out_shape=[jax.ShapeDtypeStruct((HALF, 1024), BF), jax.ShapeDtypeStruct((8, TILE), F32)],
        compiler_params=params(12),
        cost_estimate=pl.CostEstimate(flops=0, bytes_accessed=4_000_000, transcendentals=0),
        name="unturn_activation",
    )(core, mine, other)


def hand_kernel(*refs):
    pass


def hand_on(value, after):
    return pl.pallas_call(
        hand_kernel,
        in_specs=[HBM] * (1 + len(after)),
        out_specs=HBM,
        out_shape=jax.ShapeDtypeStruct(value.shape, value.dtype),
        input_output_aliases={0: 0},
        compiler_params=params(16),
        cost_estimate=pl.CostEstimate(flops=0, bytes_accessed=0, transcendentals=0),
        name="hand_on",
    )(value, *after)


def layer_kernel(
    place_ref, agg_mine, agg_other, own_mine, own_other, n0, n1, n2, n3, s0, s1, s2, s3, bias_ref,
    cot_mine, cot_other, act_mine, act_other, grad_hbm, nodes, weights, cot, act, grads, in_sems, out_sems,
):
    core, x, y = place_ref[0], place_ref[1], place_ref[2]
    here = pl.ds(pl.multiple_of(core * HALF, HALF), HALF)
    there = pl.ds(pl.multiple_of((1 - core) * HALF, HALF), HALF)
    pairs = []
    for first, second, at in ((agg_mine, own_mine, core), (agg_other, own_other, 1 - core)):
        pairs.append((first.at[:, :, pl.ds(0, HALF)], nodes.at[at, :, :, pl.ds(0, HALF)]))
        pairs.append((second.at[:, :, pl.ds(CHIP, HALF)], nodes.at[at, :, :, pl.ds(HALF, HALF)]))
        pairs.append((second.at[:, :, pl.ds(0, CHIP)], nodes.at[2 + at]))
    for far, (over_y, over_x) in enumerate(zip((n0, n1, n2, n3), (s0, s1, s2, s3))):
        for near in range(4):
            from_y, from_x = lax.rem(y - far + NY, NY) * NX + near, near * NX + lax.rem(x - far + NX, NX)
            for half, ref, block in ((0, over_y, from_y), (1, over_x, from_x)):
                pairs.append((ref.at[near], weights.at[block, :, pl.ds(half * 768, 768)]))
    pairs += [
        (cot_mine, cot.at[:, here]),
        (cot_other, cot.at[:, there]),
    ]
    copies = [pltpu.make_async_copy(src, dst, in_sems.at[i]) for i, (src, dst) in enumerate(pairs)]
    for copy in copies:
        copy.start()
    for copy in copies:
        copy.wait()
    held = nodes[...].reshape(1536, CHIP)
    rows = HALF // 2
    sent = []

    def send(src, dst):
        sent.append(pltpu.make_async_copy(src, dst, out_sems.at[len(sent)]))
        sent[-1].start()

    for chunk in range(2):
        at = pl.ds(chunk * rows, rows)
        own_weights = weights[chunk * 8 : (chunk + 1) * 8].reshape(rows, 1536)
        v = jnp.dot(own_weights, held, preferred_element_type=F32) + bias_ref[at, :]
        sq = v * v
        t = jnp.tanh(GATE * (v + CUBE * (sq * v)))
        half = 0.5 * (1.0 + t)
        act[at, :] = (v * half).astype(BF)
        send(act.at[at, here], act_mine.at[at])
        send(act.at[at, there], act_other.at[at])
        slope = half + (0.5 * GATE) * v * (1.0 - t * t) * (1.0 + (3.0 * CUBE) * sq)
        grad = (cot[at, :].astype(F32) * slope).astype(BF)
        grads[chunk * 8 : (chunk + 1) * 8] = nt(grad, held).astype(BF).reshape(8, PIECE, 1536)
        for part in range(2):
            for side in range(NC):
                src = grads.at[pl.ds(chunk * 8, 8), :, pl.ds((part * NC + side) * 384, 384)]
                send(src, grad_hbm.at[pl.ds(chunk * 8, 8), side, :, pl.ds(part * 384, 384)])
    for copy in sent:
        copy.wait()


def layer(place, aggs, owns, weights, bias, cots):
    half = jax.ShapeDtypeStruct((HALF, HALF), BF)
    return pl.pallas_call(
        layer_kernel,
        in_specs=[SMEM] + [HBM] * 12 + [VMEM] + [HBM] * 2,
        out_specs=[HBM] * 3,
        out_shape=[half, half, jax.ShapeDtypeStruct((16, NC, PIECE, 768), BF)],
        scratch_shapes=[
            pltpu.VMEM((4, NZ, COLS, CHIP), BF),
            pltpu.VMEM((16, PIECE, 1536), BF),
            pltpu.VMEM((HALF, CHIP), BF),
            pltpu.VMEM((HALF, CHIP), BF),
            pltpu.VMEM((16, PIECE, 1536), BF),
            pltpu.SemaphoreType.DMA((40,)),
            pltpu.SemaphoreType.DMA((12,)),
        ],
        compiler_params=params(56),
        cost_estimate=pl.CostEstimate(flops=3_200_000_000, bytes_accessed=9_000_000, transcendentals=524288),
        name="layer",
    )(place, *aggs, *owns, *weights, bias, *cots)


def add_kernel(in_ref, token_ref, out_ref):
    totals = [None, None]
    for i in range(32):
        term = in_ref[i].astype(F32)
        totals[i % 2] = term if totals[i % 2] is None else totals[i % 2] + term
    total = jnp.concatenate(totals, axis=0)
    for z in range(NZ):
        cut = [total[:, (part * NZ + z) * COLS :][:, :COLS] for part in range(2)]
        out_ref[z] = jnp.concatenate(cut, axis=1).astype(BF)


def add_pieces(pieces, token):
    return pl.pallas_call(
        add_kernel,
        in_specs=[VMEM, ANY],
        out_specs=VMEM,
        out_shape=jax.ShapeDtypeStruct((NZ, 64, 2 * COLS), BF),
        compiler_params=params(8),
        cost_estimate=pl.CostEstimate(flops=800_000, bytes_accessed=1_700_000, transcendentals=0),
        name="add_pieces",
    )(pieces, token)


def last_kernel(in_ref, neigh_ref, self_ref):
    total = in_ref[0].astype(F32)
    for z in range(1, NZ):
        total = total + in_ref[z].astype(F32)
    turned = total.T
    neigh_ref[...] = turned[:COLS]
    self_ref[...] = turned[COLS:]


def add_last(pieces):
    shape = jax.ShapeDtypeStruct((COLS, 64), F32)
    return pl.pallas_call(
        last_kernel,
        in_specs=[VMEM],
        out_specs=[VMEM, VMEM],
        out_shape=[shape, shape],
        compiler_params=params(8),
        cost_estimate=pl.CostEstimate(flops=50_000, bytes_accessed=200_000, transcendentals=0),
        name="add_last",
    )(pieces)


def swap(value):
    return lax.ppermute(value, "core", [(0, 1), (1, 0)])


def spread_ring(value, axis, size):
    return [value] + [
        lax.ppermute(value, axis, [(i, (i + s) % size) for i in range(size)]) for s in range(1, size)
    ]


def shards(features, target_ids, tile_index, tile_count, tile_values, w_neigh, w_self, bias, cotangent):
    core, x, y = lax.axis_index("core"), lax.axis_index("x"), lax.axis_index("y")
    core_at = core.astype(jnp.int32).reshape(1)
    place = jnp.stack([core, x, y]).astype(jnp.int32)
    feat_t = features.T

    bias_here = lax.dynamic_index_in_dim(bias.reshape(16, NC, PIECE), core, 1, keepdims=False).reshape(HALF, 1)

    agg_sent = aggregate(0, feat_t, tile_index.T, tile_count, tile_values, (w_neigh, w_self))
    agg = lax.all_to_all(agg_sent, "z", 0, 0)
    agg_late = aggregate(1, feat_t, tile_index.T, tile_count, tile_values, (agg_sent,))
    own_sent = own(feat_t, target_ids, agg_late)
    own_rows = lax.all_to_all(own_sent, "z", 0, 0)

    agg = hand_on(agg, (own_sent,))
    agg_swapped = swap(agg)
    w_n, w_s = pick_weights(core_at, agg, agg_swapped)
    weights = spread_ring(w_n, "y", NY) + spread_ring(w_s, "x", NX)

    there = sum(w[0, :8, :TILE] for w in weights[1:4] + weights[5:])
    cot_mine, cot_other = turn(core_at, cotangent, there)
    cot_swapped = swap(cot_other)
    own_rows = hand_on(own_rows, (there + cot_other[:8, :TILE], bias_here, place))
    act_mine, act_other, grads = layer(
        place, (agg, agg_swapped), (own_rows, swap(own_rows)), weights, bias_here, (cot_mine, cot_swapped)
    )
    pieces = lax.all_to_all(grads.reshape(32, PIECE, 768), ("y", "x", "core"), 0, 0)
    activation, token = unturn(core_at, act_mine, swap(act_other))
    summed = add_pieces(pieces, token)
    return activation, *add_last(lax.all_to_all(summed, "z", 0, 0))


def solution(mesh):
    split = Mesh(mesh.devices.reshape(NY, NX, NZ, NC), ("y", "x", "z", "core"))
    dp, feat = ("y", "x"), ("z", "core")
    every = dp + feat
    placed = (
        P(dp, feat), P(dp), P(dp, None), P(dp), P(dp, None, None, None),
        P(feat, None), P(feat, None), P(), P(every, None),
    )
    return jax.shard_map(
        shards,
        mesh=split,
        in_specs=placed,
        out_specs=(P(every, None), P(feat, dp), P(feat, dp)),
        check_vma=False,
    )
```
